128 devices in a mesh: dom: 128 (over z, y, x, core).
Axes of the slice: x: 4, y: 4, z: 4, core: 2. Of those that a mesh axis runs over, the one named last changes fastest.
Arguments:
- fine_state: float32 [20, 9, 16384], P(None, None, 'dom'), may hold values from -6 to 6
- coarse_state: float32 [20, 9, 32768], P(None, None, 'dom'), may hold values from -6 to 6
- fine_star: float32 [3, 9, 9, 16384], P(None, None, None, 'dom'), may hold values from -2 to 2
- coarse_star: float32 [3, 9, 9, 32768], P(None, None, None, 'dom'), may hold values from -2 to 2
- fine_flux: float32 [2, 4, 9, 9, 16384], P(None, None, None, None, 'dom'), may hold values from -2 to 2
- coarse_flux: float32 [2, 4, 9, 9, 32768], P(None, None, None, None, 'dom'), may hold values from -2 to 2
- fine_neighbors: int32 [4, 16384], P(None, 'dom'), may hold values from 0 to 527
- fine_faces: int32 [4, 16384], P(None, 'dom'), may hold values from 0 to 3
- fine_turns: int32 [4, 16384], P(None, 'dom'), may hold values from 0 to 2
- coarse_neighbors: int32 [4, 32768], P(None, 'dom'), may hold values from 0 to 527
- coarse_faces: int32 [4, 32768], P(None, 'dom'), may hold values from 0 to 3
- coarse_turns: int32 [4, 32768], P(None, 'dom'), may hold values from 0 to 2
- fine_count: int32 [128], P('dom'), may hold values from 1 to 128, 8192 in all
- send_fine: int32 [128, 12, 8], P('dom'), may hold values from 0 to 127
- send_coarse: int32 [128, 12, 4], P('dom'), may hold values from 0 to 255
- stiff_time: float32 [3, 20, 20], replicated, may hold values from -1.25 to 1.25
- stiff_volume: float32 [3, 20, 20], replicated, may hold values from -1.25 to 1.25
- face_lift: float32 [4, 20, 6], replicated, may hold values from -2.5 to 2.5
- face_project: float32 [4, 6, 20], replicated, may hold values from -1.25 to 1.25
- face_rotate: float32 [3, 6, 6], replicated, may hold values from -2.5 to 2.5
Outputs:
- fine_result: float32 [20, 9, 16384], P(None, None, 'dom')
- coarse_result: float32 [20, 9, 32768], P(None, None, 'dom')
The draws below stay inside these ranges and needn't reach their ends.
Inputs may be any that keep to these rules, and one draw needn't show every extreme that they name: `fine_count`: fine elements occupy the leading slots of each block; some block is full. `fine_neighbors`: indices into the partition's neighbour table of 528 entries. `coarse_neighbors`: indices into the partition's neighbour table of 528 entries. `send_fine`: local fine slot numbers of the sending partition. `send_coarse`: local coarse element numbers of the sending partition.
All inputs are finite; a program needn't handle non-finite values.
Results may differ from the reference program's by a relative error of at most 0.0001.
Values sent between devices are 32-bit elements; how exact they have to be, the bound alone decides.
No kernel may reach another device: no remote copies, remote signals or barrier semaphores. Data moves between devices by JAX's collectives and lax.ppermute only.
A program may use at most 128 MiB of HBM per device.

```python
import math
from functools import reduce
import jax
import jax.numpy as jnp
import numpy as np
from jax import lax

NB = 20
NQ = 9
FACE_NB = 6
REACH = 6
FINE_CAP = 128
COARSE_DEV = 256
S_FINE = 8
S_COARSE = 4
POOL = 528
FINE_TOTAL = 16384
COARSE_TOTAL = 32768
N_DOM = 128


def touch_ends(result, stream_key, least, top_value):
    longest = result.shape.index(max(result.shape))
    spots = []
    for shift in (0, 1):
        where = [jax.random.randint(jax.random.fold_in(stream_key, axis), (), 0, length) for axis, length in enumerate(result.shape)]
        where[longest] = (where[longest] + shift) % result.shape[longest]
        spots.append(tuple(where))
    return result.at[spots[0]].set(least).at[spots[1]].set(top_value)


def block_levels(key, shape, cuts, low, largest):
    def one(axis_at, shards_of):
        steps = jax.random.uniform(jax.random.fold_in(jax.random.fold_in(key, 6), axis_at), (shards_of,), jnp.float32, low / len(cuts), largest / len(cuts))
        return jnp.repeat(jnp.exp(steps), shape[axis_at] // shards_of).reshape((-1,) + (1,) * (len(shape) - axis_at - 1))

    factor_of = one(*cuts[0])
    for cut in cuts[1:]:
        factor_of = factor_of * one(*cut)
    return factor_of


def length_profile(number_of, total, most, lean):
    loads = [(1 << 20) // math.isqrt(grade ** lean) + 1 for grade in range(2, number_of + 1)]
    surplus, holding = total - most - (number_of - 1), [1] * (number_of - 1)
    while surplus > 0:
        free = [i for i in range(number_of - 1) if holding[i] < most]
        whole, budget = sum([loads[i] for i in free]), surplus
        for i in free:
            more = min(most - holding[i], max(1, budget * loads[i] // whole), surplus)
            holding[i] = holding[i] + more
            surplus = surplus - more
    return np.array([most] + holding)


def ragged(stream_key, amount, total, bound, skew):
    if amount == 2:
        one = jax.random.randint(stream_key, (), max(1, total - bound), min(bound, total - 1) + 1)
        return jnp.stack([one, total - one])
    tallies = jnp.asarray(length_profile(amount, total, bound, skew), jnp.int32)
    twos = (amount - 1) // 2
    giver, sink = tallies[1:1 + 2 * twos:2], tallies[2:2 + 2 * twos:2]
    slack = jnp.minimum(giver - 1, bound - sink)
    moved = jax.random.randint(jax.random.fold_in(stream_key, 1), (twos,), 0, 1 << 20) % (slack + 1)
    tallies = tallies.at[1:1 + 2 * twos:2].set(giver - moved).at[2:2 + 2 * twos:2].set(sink + moved)
    return tallies[jax.random.permutation(jax.random.fold_in(stream_key, 2), amount)]


def gaussian(own_key, extent, width, reach, cuts=(), held_as=jnp.bfloat16):
    result = jax.random.normal(own_key, extent, jnp.float32) * width
    if len(cuts) > 0:
        result = block_levels(own_key, extent, cuts, -0.22, 0.18) * result
    return jnp.clip(result, min=-reach, max=reach).astype(held_as)


def setup_inputs(seed: int = 0) -> dict:
    keys = jax.random.split(jax.random.key(seed), 21)
    return {
        "fine_state": gaussian(keys[0], (NB, NQ, FINE_TOTAL), 1.0, 6.0, ((2, 128),), jnp.float32),
        "coarse_state": gaussian(keys[1], (NB, NQ, COARSE_TOTAL), 1.0, 6.0, ((2, 128),), jnp.float32),
        "fine_star": gaussian(keys[2], (3, NQ, NQ, FINE_TOTAL), NQ ** -0.5, 2.0, ((3, 128),), jnp.float32),
        "coarse_star": gaussian(keys[3], (3, NQ, NQ, COARSE_TOTAL), NQ ** -0.5, 2.0, ((3, 128),), jnp.float32),
        "fine_flux": gaussian(keys[4], (2, 4, NQ, NQ, FINE_TOTAL), NQ ** -0.5, 2.0, ((4, 128),), jnp.float32),
        "coarse_flux": gaussian(keys[5], (2, 4, NQ, NQ, COARSE_TOTAL), NQ ** -0.5, 2.0, ((4, 128),), jnp.float32),
        "fine_neighbors": touch_ends(jax.random.randint(keys[6], (4, FINE_TOTAL), 0, POOL), jax.random.fold_in(keys[6], 1), 0, POOL - 1).astype(jnp.int32),
        "fine_faces": touch_ends(jax.random.randint(keys[7], (4, FINE_TOTAL), 0, 4), jax.random.fold_in(keys[7], 1), 0, 3).astype(jnp.int32),
        "fine_turns": touch_ends(jax.random.randint(keys[8], (4, FINE_TOTAL), 0, 3), jax.random.fold_in(keys[8], 1), 0, 2).astype(jnp.int32),
        "coarse_neighbors": touch_ends(jax.random.randint(keys[9], (4, COARSE_TOTAL), 0, POOL), jax.random.fold_in(keys[9], 1), 0, POOL - 1).astype(jnp.int32),
        "coarse_faces": touch_ends(jax.random.randint(keys[10], (4, COARSE_TOTAL), 0, 4), jax.random.fold_in(keys[10], 1), 0, 3).astype(jnp.int32),
        "coarse_turns": touch_ends(jax.random.randint(keys[11], (4, COARSE_TOTAL), 0, 3), jax.random.fold_in(keys[11], 1), 0, 2).astype(jnp.int32),
        "fine_count": ragged(keys[12], N_DOM, N_DOM * FINE_CAP // 2, FINE_CAP, 2).astype(jnp.int32),
        "send_fine": touch_ends(jax.random.randint(keys[13], (N_DOM, 2 * REACH, S_FINE), 0, FINE_CAP), jax.random.fold_in(keys[13], 1), 0, FINE_CAP - 1).astype(jnp.int32),
        "send_coarse": touch_ends(jax.random.randint(keys[14], (N_DOM, 2 * REACH, S_COARSE), 0, COARSE_DEV), jax.random.fold_in(keys[14], 1), 0, COARSE_DEV - 1).astype(jnp.int32),
        "stiff_time": gaussian(keys[15], (3, NB, NB), NB ** -0.5, 1.25, (), jnp.float32),
        "stiff_volume": gaussian(keys[16], (3, NB, NB), NB ** -0.5, 1.25, (), jnp.float32),
        "face_lift": gaussian(keys[17], (4, NB, FACE_NB), FACE_NB ** -0.5, 2.5, (), jnp.float32),
        "face_project": gaussian(keys[18], (4, FACE_NB, NB), NB ** -0.5, 1.25, (), jnp.float32),
        "face_rotate": gaussian(keys[19], (3, FACE_NB, FACE_NB), FACE_NB ** -0.5, 2.5, (), jnp.float32),
    }


FIRST_HALF = (0.5, 0.125, 1.0 / 48.0)
SECOND_HALF = (0.5, 0.375, 7.0 / 48.0)


def peer_offsets():
    return list(range(-REACH, 0)) + list(range(1, REACH + 1))


def basis_apply(matrix, field):
    return jnp.einsum('ab,bqe->aqe', matrix, field, precision=lax.Precision.HIGHEST)


def star_apply(field, star):
    return jnp.einsum('bqe,qpe->bpe', field, star, precision=lax.Precision.HIGHEST)


def derivatives(state, star, stiff):
    terms = [state]
    for k in range(2):
        prior = terms[-1]
        parts = [star_apply(basis_apply(stiff[d], prior), star[d]) for d in range(3)]
        terms.append(-reduce(jnp.add, parts))
    return terms


def integrate(terms, weights):
    return reduce(jnp.add, [w * t for w, t in zip(weights, terms)])


def correct(state, integral, table, neighbors, faces, turns, star, flux, stiff_volume, face_lift, face_project, face_rotate):
    volume = [star_apply(basis_apply(stiff_volume[d], integral), star[d]) for d in range(3)]
    updated = state + reduce(jnp.add, volume)
    for i in range(4):
        own_side = star_apply(basis_apply(face_project[i], integral), flux[0, i])
        updated = updated + basis_apply(face_lift[i], own_side)
        other = jnp.take(table, neighbors[i], axis=2)
        picked = reduce(jnp.add, [jnp.where(faces[i] == j, basis_apply(face_project[j], other), 0.0) for j in range(4)])
        turned = reduce(jnp.add, [jnp.where(turns[i] == h, basis_apply(face_rotate[h], picked), 0.0) for h in range(3)])
        updated = updated + basis_apply(face_lift[i], star_apply(turned, flux[1, i]))
    return updated


def ghost_rows(data, send_rows, block):
    offsets = jnp.array(peer_offsets(), dtype=jnp.int32)
    device = jnp.arange(N_DOM, dtype=jnp.int32)[:, None]
    source = device - offsets[None, :]
    inside = (source >= 0) & (source < N_DOM)
    clipped = jnp.clip(source, 0, N_DOM - 1).astype(jnp.int32)
    chosen = send_rows[clipped, jnp.arange(2 * REACH, dtype=jnp.int32)[None, :]]
    index = (clipped[:, :, None] * block + chosen).reshape(-1).astype(jnp.int32)
    taken = jnp.take(data, index, axis=2).reshape(NB, NQ, N_DOM, 2 * REACH, -1)
    taken = jnp.where(inside[None, None, :, :, None], taken, 0.0)
    return taken.reshape(NB, NQ, -1)


def build_table(parts):
    pieces = [p.reshape(NB, NQ, N_DOM, -1) for p in parts]
    return jnp.concatenate(pieces, axis=3).reshape(NB, NQ, -1)


def table_index(neighbors, block):
    owner = (jnp.arange(neighbors.shape[1], dtype=jnp.int32) // block).astype(jnp.int32)
    return (owner[None, :] * POOL + neighbors).astype(jnp.int32)


def reference(fine_state, coarse_state, fine_star, coarse_star, fine_flux, coarse_flux, fine_neighbors, fine_faces, fine_turns, coarse_neighbors, coarse_faces, coarse_turns, fine_count, send_fine, send_coarse, stiff_time, stiff_volume, face_lift, face_project, face_rotate):
    slots = jnp.arange(FINE_TOTAL, dtype=jnp.int32)
    live = (slots % FINE_CAP) < jnp.repeat(fine_count, FINE_CAP)
    coarse_terms = derivatives(coarse_state, coarse_star, stiff_time)
    coarse_first = integrate(coarse_terms, FIRST_HALF)
    coarse_second = integrate(coarse_terms, SECOND_HALF)
    coarse_full = coarse_first + coarse_second
    ghost_first = ghost_rows(coarse_first, send_coarse, COARSE_DEV)
    ghost_second = ghost_rows(coarse_second, send_coarse, COARSE_DEV)
    ghost_full = ghost_first + ghost_second
    coarse_halves = [coarse_first, coarse_second]
    ghost_halves = [ghost_first, ghost_second]
    fine_index = table_index(fine_neighbors, FINE_CAP)
    state = fine_state
    integrals = []
    fine_ghost = []
    for step in range(2):
        terms = derivatives(state, fine_star, stiff_time)
        integral = jnp.where(live, integrate(terms, FIRST_HALF), 0.0)
        ghosts = ghost_rows(integral, send_fine, FINE_CAP)
        table = build_table([integral, coarse_halves[step], ghosts, ghost_halves[step]])
        updated = correct(state, integral, table, fine_index, fine_faces, fine_turns, fine_star, fine_flux, stiff_volume, face_lift, face_project, face_rotate)
        state = jnp.where(live, updated, state)
        integrals.append(integral)
        fine_ghost.append(ghosts)
    table = build_table([integrals[0] + integrals[1], coarse_full, fine_ghost[0] + fine_ghost[1], ghost_full])
    coarse_index = table_index(coarse_neighbors, COARSE_DEV)
    coarse_result = correct(coarse_state, coarse_full, table, coarse_index, coarse_faces, coarse_turns, coarse_star, coarse_flux, stiff_volume, face_lift, face_project, face_rotate)
    return state, coarse_result
```

```python
from functools import partial

import jax
import jax.numpy as jnp
from jax import lax
from jax.experimental import pallas as pl
from jax.experimental.pallas import tpu as pltpu
from jax.sharding import PartitionSpec as P

NB = 20
NQ = 9
FNB = 6
REACH = 6
BP = 24
FP = 8
LANES = 128
ROW = 384
FIRST_HALF = (0.5, 0.125, 1.0 / 48.0)
SECOND_HALF = (0.5, 0.375, 7.0 / 48.0)
F32 = jnp.float32
BF16 = jnp.bfloat16
I32 = jnp.int32
N_DEV = 128


def halves(x):
    hi = x.astype(BF16).astype(F32)
    return hi, x - hi


def stacked(x):
    hi, lo = halves(x)
    return jnp.concatenate([hi, lo, hi], axis=0).astype(BF16)


def fill_weight(ref, blocks, row_step, col_step):
    ref[...] = jnp.zeros(ref.shape, F32)
    for i, block in enumerate(blocks):
        rows, cols = block.shape
        hi, lo = halves(block)
        span = slice(i * row_step, i * row_step + rows)
        ref[span, 0:cols] = hi
        ref[span, col_step : col_step + cols] = hi
        ref[span, 2 * col_step : 2 * col_step + cols] = lo


def weight(ref, depth):
    return ref[:, 0 : 3 * depth].astype(BF16)


def mm(w, x):
    return jnp.dot(w, stacked(x), preferred_element_type=F32)


def load_state(state_ref, x_ref, width):
    for q in range(NQ):
        x_ref[NB:BP, q * width : (q + 1) * width] = jnp.zeros((BP - NB, width), F32)
        x_ref[0:NB, q * width : (q + 1) * width] = state_ref[:, q, :]


def star_sum(t_ref, star_ref, width, tile):
    lanes = slice(tile * LANES, (tile + 1) * LANES)
    acc = [None] * NQ
    for d in range(3):
        for q in range(NQ):
            t = t_ref[d * BP : (d + 1) * BP, q * width + tile * LANES : q * width + (tile + 1) * LANES]
            for p in range(NQ):
                term = t * star_ref[d, q, p : p + 1, lanes]
                acc[p] = term if acc[p] is None else acc[p] + term
    return acc


def put(ref, values, width, tile):
    for p in range(NQ):
        ref[:, p * width + tile * LANES : p * width + (tile + 1) * LANES] = values[p]


def get(ref, width, tile):
    return [
        ref[:, p * width + tile * LANES : p * width + (tile + 1) * LANES] for p in range(NQ)
    ]


def predictor(x_ref, d_ref, t_ref, star_ref, w, width, emit):
    tiles = width // LANES
    t_ref[...] = mm(w, x_ref[...])
    for tile in range(tiles):
        put(d_ref, star_sum(t_ref, star_ref, width, tile), width, tile)
    t_ref[...] = mm(w, d_ref[...])
    for tile in range(tiles):
        second = star_sum(t_ref, star_ref, width, tile)
        emit(tile, get(x_ref, width, tile), get(d_ref, width, tile), second)


def combine(weights, state, neg_first, second):
    return [
        weights[0] * s - weights[1] * f + weights[2] * g
        for s, f, g in zip(state, neg_first, second)
    ]


def place():
    me = lax.axis_index("dom").astype(I32)
    return me, me >> 1, me & 1


def route(plane, pos, rel):
    me, chip, core = place()
    even = ((chip >> 3) << 3) + pos
    odd = (((chip + 4) >> 3) << 3) - 4 + ((pos + 4) & 7)
    target = jnp.where(plane == 0, even, odd)
    cross = (target >> 3) != (chip >> 3)
    other = (rel ^ plane)
    offset = 2 * (target - chip) + other - core
    valid = (target >= 0) & (target < N_DEV // 2) & (offset >= -REACH) & (offset <= REACH)
    valid = valid & (offset != 0) & ((plane == 0) | cross)
    peer = jnp.where(offset < 0, offset + REACH, offset + REACH - 1)
    return jnp.clip(peer, 0, 2 * REACH - 1), valid


def picker(send_ref, plane, width, slots):
    rows = []
    for m in range(16):
        peer, valid = route(plane, m // 2, m % 2)
        row = send_ref[0, pl.ds(peer, 1), :]
        rows.append(jnp.broadcast_to(jnp.where(valid, row, -1), (8, width)))
    big = jnp.concatenate(rows, axis=0).astype(F32)
    s = lax.broadcasted_iota(I32, (LANES, width), 0) & (width - 1)
    lane = lax.broadcasted_iota(I32, (LANES, width), 1)
    index = jnp.sum(jnp.where(lane == s, big, 0.0), axis=1, keepdims=True)
    slot = lax.broadcasted_iota(I32, (LANES, slots), 1).astype(F32)
    return jnp.where(slot == index, 1.0, 0.0).astype(BF16)


def rows_of(ref, width, first, last):
    return jnp.concatenate([ref[:, q * width : (q + 1) * width] for q in range(first, last)], axis=0)


def picked(hot, field):
    hi, lo = halves(field)
    both = jnp.concatenate([hi, lo], axis=1).astype(BF16)
    hots = jnp.concatenate([hot, hot], axis=1)
    return lax.dot_general(hots, both, (((1,), (1,)), ((), ())), preferred_element_type=F32)


def pack(out_ref, plane, fine_ref, coarse_ref, send_fine_ref, send_coarse_ref):
    hot = picker(send_fine_ref, plane, 8, LANES)
    out_ref[:, 0:256] = jnp.zeros((LANES, 256), F32)
    out_ref[:, 0 : NQ * BP] = picked(hot, rows_of(fine_ref, LANES, 0, NQ))
    hot = picker(send_coarse_ref, plane, 4, 2 * LANES)
    low = picked(hot, rows_of(coarse_ref, 2 * LANES, 0, 5))
    high = picked(hot, rows_of(coarse_ref, 2 * LANES, 5, NQ))
    high = jnp.concatenate([high, jnp.zeros((LANES, BP), F32)], axis=1)
    s = lax.broadcasted_iota(I32, (LANES, 5 * BP), 0) & 7
    out_ref[:, 256:ROW] = jnp.zeros((LANES, LANES), F32)
    out_ref[:, 256 : 256 + 5 * BP] = jnp.where(s < 4, low, high)


def unpack(mine_ref, back_ref, prior, fine_ref, coarse_ref):
    parts = []
    for i in range(8):
        for rel in range(2):
            parts.append(mine_ref[i, rel, 0] + back_ref[i, 1 - rel])
    rows = jnp.concatenate(parts, axis=0)
    turned = [rows[:, t * LANES : (t + 1) * LANES].T for t in range(3)]
    fine = jnp.concatenate(turned[:2], axis=0)
    coarse = turned[2]
    for q in range(NQ):
        fine_ref[:, q * LANES : (q + 1) * LANES] = fine[q * BP : (q + 1) * BP]
        at = (q % 5) * BP
        coarse_ref[:, q * LANES : (q + 1) * LANES] = coarse[at : at + BP]


def first_kernel(
    fine_state, fine_star, coarse_state, coarse_star, count, send_fine, send_coarse, stiff,
    keep, swap, x_fine, i_fine, x_coarse, c_first, c_second,
    w_ref, d_fine, t_fine, d_coarse, t_coarse,
):
    fill_weight(w_ref, [stiff[d] for d in range(3)], BP, BP)
    w = weight(w_ref, BP)
    load_state(coarse_state, x_coarse, 2 * LANES)
    load_state(fine_state, x_fine, LANES)

    def emit_coarse(tile, *terms):
        put(c_first, combine(FIRST_HALF, *terms), 2 * LANES, tile)
        put(c_second, combine(SECOND_HALF, *terms), 2 * LANES, tile)

    live = lax.broadcasted_iota(I32, (BP, LANES), 1) < count[0]

    def emit_fine(tile, *terms):
        values = combine(FIRST_HALF, *terms)
        put(i_fine, [jnp.where(live, v, 0.0) for v in values], LANES, tile)

    predictor(x_coarse, d_coarse, t_coarse, coarse_star, w, 2 * LANES, emit_coarse)
    predictor(x_fine, d_fine, t_fine, fine_star, w, LANES, emit_fine)
    core = place()[2]
    pack(keep, core, i_fine, c_first, send_fine, send_coarse)
    pack(swap, 1 - core, i_fine, c_first, send_fine, send_coarse)


def locate(n):
    me, _, core = place()
    local = n < 384
    fine = n < 480
    g = jnp.where(fine, n - 384, n - 480)
    j = jnp.where(fine, g >> 3, g >> 2)
    s = jnp.where(fine, g & 7, g & 3)
    offset = j - REACH + jnp.where(j >= REACH, 1, 0)
    block = ((me - offset) & 15) ^ core
    lane = jnp.where(local, n & 127, block * 8 + s)
    tile = jnp.where(local, n >> 7, jnp.where(fine, 3, 4))
    return tile, lane


def correct(
    state_ref, i_ref, width, tables, neighbors, faces, turns, star_ref, flux_ref, weights,
    p_ref, t_ref, n_ref, l_ref, emit,
):
    w_vol, w_proj, w_rot, w_lift = weights
    p_ref[...] = mm(w_proj, i_ref[...])
    t_ref[...] = mm(w_vol, i_ref[...])
    for tile in range(width // LANES):
        lanes = slice(tile * LANES, (tile + 1) * LANES)
        for i in range(4):
            number = jnp.broadcast_to(neighbors[i : i + 1, lanes], (8, LANES))
            where_tile, lane = locate(number)
            later = jnp.where(where_tile == 4, lane + 4, lane)
            masks = [where_tile == k for k in range(5)]
            for q in range(NQ):
                at = lane if q < 5 else later
                for g in range(3):
                    value = None
                    for k, (ref, ref_width, ref_tile) in enumerate(tables):
                        start = q * ref_width + ref_tile * LANES
                        source = ref[8 * g : 8 * g + 8, start : start + LANES]
                        found = jnp.take_along_axis(source, at, axis=1)
                        value = found if value is None else jnp.where(masks[k], found, value)
                    n_ref[8 * g : 8 * g + 8, q * LANES : (q + 1) * LANES] = value
            projected = mm(w_proj, n_ref[...])
            face = jnp.broadcast_to(faces[i : i + 1, lanes], (FP, LANES))
            turn = jnp.broadcast_to(turns[i : i + 1, lanes], (FP, LANES))
            chosen = []
            for q in range(NQ):
                at = slice(q * LANES, (q + 1) * LANES)
                value = projected[0:FP, at]
                for f in range(1, 4):
                    value = jnp.where(face == f, projected[f * FP : (f + 1) * FP, at], value)
                chosen.append(value)
            rotated = mm(w_rot, jnp.concatenate(chosen, axis=1))
            acc = [None] * NQ
            for q in range(NQ):
                at = slice(q * LANES, (q + 1) * LANES)
                other = rotated[0:FP, at]
                for h in range(1, 3):
                    other = jnp.where(turn == h, rotated[h * FP : (h + 1) * FP, at], other)
                start = q * width + tile * LANES
                own = p_ref[i * FP : (i + 1) * FP, start : start + LANES]
                for p in range(NQ):
                    term = own * flux_ref[0, i, q, p : p + 1, lanes]
                    term = term + other * flux_ref[1, i, q, p : p + 1, lanes]
                    acc[p] = term if acc[p] is None else acc[p] + term
            for p in range(NQ):
                l_ref[i * FP : (i + 1) * FP, p * LANES : (p + 1) * LANES] = acc[p]
        lifted = mm(w_lift, l_ref[...])
        volume = star_sum(t_ref, star_ref, width, tile)
        state = get(state_ref, width, tile)
        emit(
            tile,
            [state[p] + (volume[p] + lifted[:, p * LANES : (p + 1) * LANES]) for p in range(NQ)],
        )


def fill_corrector(stiff_volume, lift, project, rotate, w_vol, w_proj, w_rot, w_lift):
    fill_weight(w_vol, [stiff_volume[d] for d in range(3)], BP, BP)
    fill_weight(w_proj, [project[f] for f in range(4)], FP, BP)
    fill_weight(w_rot, [rotate[h] for h in range(3)], FP, FP)
    w_lift[...] = jnp.zeros(w_lift.shape, F32)
    for i in range(4):
        hi, lo = halves(lift[i])
        w_lift[0:NB, i * FP : i * FP + FNB] = hi
        w_lift[0:NB, 32 + i * FP : 32 + i * FP + FNB] = hi
        w_lift[0:NB, 64 + i * FP : 64 + i * FP + FNB] = lo
    return weight(w_vol, BP), weight(w_proj, BP), weight(w_rot, FP), weight(w_lift, 32)


def second_kernel(
    mine, back, x_fine, i_fine, c_first, c_second, fine_star, fine_flux,
    neighbors, faces, turns, count, send_fine, send_coarse,
    stiff, stiff_volume, lift, project, rotate,
    keep, swap, x_next, i_next, ghost_f, ghost_c,
    w_ref, w_vol, w_proj, w_rot, w_lift, p_ref, t_ref, n_ref, l_ref, d_ref,
):
    weights = fill_corrector(stiff_volume, lift, project, rotate, w_vol, w_proj, w_rot, w_lift)
    fill_weight(w_ref, [stiff[d] for d in range(3)], BP, BP)
    unpack(mine, back, None, ghost_f, ghost_c)
    live = lax.broadcasted_iota(I32, (BP, LANES), 1) < count[0]
    tables = [
        (i_fine, LANES, 0), (c_first, 2 * LANES, 0), (c_first, 2 * LANES, 1),
        (ghost_f, LANES, 0), (ghost_c, LANES, 0),
    ]

    def emit_state(tile, values):
        old = get(x_fine, LANES, 0)
        put(x_next, [jnp.where(live, v, o) for v, o in zip(values, old)], LANES, 0)

    correct(
        x_fine, i_fine, LANES, tables, neighbors, faces, turns, fine_star, fine_flux, weights,
        p_ref, t_ref, n_ref, l_ref, emit_state,
    )

    def emit_fine(tile, *terms):
        values = combine(FIRST_HALF, *terms)
        put(i_next, [jnp.where(live, v, 0.0) for v in values], LANES, 0)

    predictor(x_next, d_ref, t_ref, fine_star, weight(w_ref, BP), LANES, emit_fine)
    core = place()[2]
    pack(keep, core, i_next, c_second, send_fine, send_coarse)
    pack(swap, 1 - core, i_next, c_second, send_fine, send_coarse)


def third_kernel(
    mine, back, x_fine, i_first, i_fine, x_coarse, c_first, c_second, g_fine, g_coarse,
    fine_star, fine_flux, coarse_star, coarse_flux,
    neighbors, faces, turns, c_neighbors, c_faces, c_turns, count,
    stiff_volume, lift, project, rotate,
    fine_out, coarse_out,
    w_vol, w_proj, w_rot, w_lift, p_ref, t_ref, n_ref, l_ref, pc_ref, tc_ref,
    ghost_f, ghost_c, c_full, i_both,
):
    weights = fill_corrector(stiff_volume, lift, project, rotate, w_vol, w_proj, w_rot, w_lift)
    unpack(mine, back, None, ghost_f, ghost_c)
    live = lax.broadcasted_iota(I32, (NB, LANES), 1) < count[0]
    tables = [
        (i_fine, LANES, 0), (c_second, 2 * LANES, 0), (c_second, 2 * LANES, 1),
        (ghost_f, LANES, 0), (ghost_c, LANES, 0),
    ]

    def emit_fine(tile, values):
        old = get(x_fine, LANES, 0)
        for p in range(NQ):
            fine_out[:, p, :] = jnp.where(live, values[p][:NB], old[p][:NB])

    correct(
        x_fine, i_fine, LANES, tables, neighbors, faces, turns, fine_star, fine_flux, weights,
        p_ref, t_ref, n_ref, l_ref, emit_fine,
    )
    c_full[...] = c_first[...] + c_second[...]
    i_both[...] = i_first[...] + i_fine[...]
    ghost_f[...] = ghost_f[...] + g_fine[...]
    ghost_c[...] = ghost_c[...] + g_coarse[...]
    tables = [
        (i_both, LANES, 0), (c_full, 2 * LANES, 0), (c_full, 2 * LANES, 1),
        (ghost_f, LANES, 0), (ghost_c, LANES, 0),
    ]

    def emit_coarse(tile, values):
        for p in range(NQ):
            coarse_out[:, p, tile * LANES : (tile + 1) * LANES] = values[p][:NB]

    correct(
        x_coarse, c_full, 2 * LANES, tables, c_neighbors, c_faces, c_turns, coarse_star,
        coarse_flux, weights, pc_ref, tc_ref, n_ref, l_ref, emit_coarse,
    )


VM = pl.BlockSpec(memory_space=pltpu.VMEM)
SM = pl.BlockSpec(memory_space=pltpu.SMEM)


def struct(*shape):
    return jax.ShapeDtypeStruct(shape, F32)


def scratch(*shape):
    return pltpu.VMEM(shape, F32)


FINE = (BP, NQ * LANES)
COARSE = (BP, 2 * NQ * LANES)
SENT = (LANES, ROW)
WEIGHTS = [(3 * BP, LANES), (4 * FP, LANES), (3 * FP, LANES), (BP, LANES)]
PARAMS = pltpu.CompilerParams(vmem_limit_bytes=24 * 1024 * 1024)


def call(kernel, name, in_specs, outs, scratches, args):
    return pl.pallas_call(
        kernel,
        name=name,
        in_specs=in_specs,
        out_specs=[VM] * len(outs),
        out_shape=[struct(*s) for s in outs],
        scratch_shapes=[scratch(*s) for s in scratches],
        compiler_params=PARAMS,
    )(*args)


def planes():
    groups = []
    for core in range(2):
        for k in range(8):
            first = [8 * k + i for i in range(8)]
            second = [(8 * k - 4 + (i + 4) % 8) % 64 for i in range(8)]
            groups.append([2 * chip + core for chip in (second if core else first)])
    return groups


SIBLING = [(i, i ^ 1) for i in range(N_DEV)]


def exchange(keep, swap):
    arrived = lax.ppermute(swap, "dom", SIBLING)
    blocks = jnp.stack([keep.reshape(8, 2, 8, ROW), arrived.reshape(8, 2, 8, ROW)], axis=1)
    got = lax.all_to_all(blocks, "dom", 0, 0, axis_index_groups=planes(), tiled=True)
    back = lax.ppermute(got[:, :, 1], "dom", SIBLING)
    return got, back


def local(
    fine_state, coarse_state, fine_star, coarse_star, fine_flux, coarse_flux,
    fine_neighbors, fine_faces, fine_turns, coarse_neighbors, coarse_faces, coarse_turns,
    fine_count, send_fine, send_coarse,
    stiff_time, stiff_volume, face_lift, face_project, face_rotate,
):
    keep, swap, x_fine, i_first, x_coarse, c_first, c_second = call(
        first_kernel, "predict",
        [VM, VM, VM, VM, SM, VM, VM, VM],
        [SENT, SENT, FINE, FINE, COARSE, COARSE, COARSE],
        [(3 * BP, LANES), FINE, (3 * BP, NQ * LANES), COARSE, (3 * BP, 2 * NQ * LANES)],
        (fine_state, fine_star, coarse_state, coarse_star, fine_count, send_fine, send_coarse,
         stiff_time),
    )
    mine, back = exchange(keep, swap)
    keep, swap, x_next, i_second, g_fine, g_coarse = call(
        second_kernel, "substep",
        [VM] * 11 + [SM] + [VM] * 7,
        [SENT, SENT, FINE, FINE, FINE, FINE],
        [(3 * BP, LANES)] + WEIGHTS
        + [(4 * FP, NQ * LANES), (3 * BP, NQ * LANES), FINE, (4 * FP, NQ * LANES), FINE],
        (mine, back, x_fine, i_first, c_first, c_second, fine_star, fine_flux,
         fine_neighbors, fine_faces, fine_turns, fine_count, send_fine, send_coarse,
         stiff_time, stiff_volume, face_lift, face_project, face_rotate),
    )
    mine, back = exchange(keep, swap)
    return tuple(call(
        third_kernel, "finish",
        [VM] * 20 + [SM] + [VM] * 4,
        [(NB, NQ, LANES), (NB, NQ, 2 * LANES)],
        WEIGHTS
        + [(4 * FP, NQ * LANES), (3 * BP, NQ * LANES), FINE, (4 * FP, NQ * LANES)]
        + [(4 * FP, 2 * NQ * LANES), (3 * BP, 2 * NQ * LANES), FINE, FINE, COARSE, FINE],
        (mine, back, x_next, i_first, i_second, x_coarse, c_first, c_second, g_fine, g_coarse,
         fine_star, fine_flux, coarse_star, coarse_flux,
         fine_neighbors, fine_faces, fine_turns, coarse_neighbors, coarse_faces, coarse_turns,
         fine_count, stiff_volume, face_lift, face_project, face_rotate),
    ))


def solution(mesh):
    placed = (
        P(None, None, "dom"),
        P(None, None, "dom"),
        P(None, None, None, "dom"),
        P(None, None, None, "dom"),
        P(None, None, None, None, "dom"),
        P(None, None, None, None, "dom"),
        P(None, "dom"),
        P(None, "dom"),
        P(None, "dom"),
        P(None, "dom"),
        P(None, "dom"),
        P(None, "dom"),
        P("dom"),
        P("dom", None, None),
        P("dom", None, None),
        P(),
        P(),
        P(),
        P(),
        P(),
    )
    return jax.shard_map(
        local,
        mesh=mesh,
        in_specs=placed,
        out_specs=(P(None, None, "dom"), P(None, None, "dom")),
        check_vma=False,
    )
```

```python
from functools import partial

import jax
import jax.numpy as jnp
from jax import lax
from jax.experimental import pallas as pl
from jax.experimental.pallas import tpu as pltpu
from jax.sharding import PartitionSpec as P

NB = 20
NQ = 9
FNB = 6
REACH = 6
BP = 24
FP = 8
LANES = 128
ROW = 384
FIRST_HALF = (0.5, 0.125, 1.0 / 48.0)
SECOND_HALF = (0.5, 0.375, 7.0 / 48.0)
F32 = jnp.float32
BF16 = jnp.bfloat16
I32 = jnp.int32
N_DEV = 128


def halves(x):
    hi = x.astype(BF16).astype(F32)
    return hi, x - hi


def stacked(x):
    hi, lo = halves(x)
    return jnp.concatenate([hi, lo, hi], axis=0).astype(BF16)


def fill_weight(ref, blocks, row_step, col_step):
    ref[...] = jnp.zeros(ref.shape, F32)
    for i, block in enumerate(blocks):
        rows, cols = block.shape
        hi, lo = halves(block)
        span = slice(i * row_step, i * row_step + rows)
        ref[span, 0:cols] = hi
        ref[span, col_step : col_step + cols] = hi
        ref[span, 2 * col_step : 2 * col_step + cols] = lo


def weight(ref, depth):
    return ref[:, 0 : 3 * depth].astype(BF16)


def mm(w, x):
    return jnp.dot(w, stacked(x), preferred_element_type=F32)


def load_state(state_ref, x_ref, width):
    for q in range(NQ):
        x_ref[NB:BP, q * width : (q + 1) * width] = jnp.zeros((BP - NB, width), F32)
        x_ref[0:NB, q * width : (q + 1) * width] = state_ref[q]


def star_sum(t_ref, star_ref, width, tile):
    lanes = slice(tile * LANES, (tile + 1) * LANES)
    acc = [None] * NQ
    for d in range(3):
        for q in range(NQ):
            t = t_ref[d * BP : (d + 1) * BP, q * width + tile * LANES : q * width + (tile + 1) * LANES]
            for p in range(NQ):
                term = t * star_ref[q, p, d : d + 1, lanes]
                acc[p] = term if acc[p] is None else acc[p] + term
    return acc


def put(ref, values, width, tile):
    for p in range(NQ):
        ref[:, p * width + tile * LANES : p * width + (tile + 1) * LANES] = values[p]


def get(ref, width, tile):
    return [
        ref[:, p * width + tile * LANES : p * width + (tile + 1) * LANES] for p in range(NQ)
    ]


def predictor(x_ref, d_ref, t_ref, star_ref, w, width, emit):
    tiles = width // LANES
    t_ref[...] = mm(w, x_ref[...])
    for tile in range(tiles):
        put(d_ref, star_sum(t_ref, star_ref, width, tile), width, tile)
    t_ref[...] = mm(w, d_ref[...])
    for tile in range(tiles):
        second = star_sum(t_ref, star_ref, width, tile)
        emit(tile, get(x_ref, width, tile), get(d_ref, width, tile), second)


def combine(weights, state, neg_first, second):
    return [
        weights[0] * s - weights[1] * f + weights[2] * g
        for s, f, g in zip(state, neg_first, second)
    ]


def place():
    me = lax.axis_index("dom").astype(I32)
    return me, me >> 1, me & 1


def route(plane, pos, rel):
    me, chip, core = place()
    even = ((chip >> 3) << 3) + pos
    odd = (((chip + 4) >> 3) << 3) - 4 + ((pos + 4) & 7)
    target = jnp.where(plane == 0, even, odd)
    cross = (target >> 3) != (chip >> 3)
    other = (rel ^ plane)
    offset = 2 * (target - chip) + other - core
    valid = (target >= 0) & (target < N_DEV // 2) & (offset >= -REACH) & (offset <= REACH)
    valid = valid & (offset != 0) & ((plane == 0) | cross)
    peer = jnp.where(offset < 0, offset + REACH, offset + REACH - 1)
    return jnp.clip(peer, 0, 2 * REACH - 1), valid


def picker(send_ref, plane, slots):
    table = send_ref[0].astype(F32) + 1.0
    if table.shape[0] < 8:
        table = jnp.concatenate([table, table], axis=0)
    lane = lax.broadcasted_iota(I32, table.shape, 1)
    rows = []
    for m in range(16):
        peer, valid = route(plane, m // 2, m % 2)
        rows.append(jnp.where(lane == jnp.where(valid, peer, -1), table, 0.0))
    index = jnp.sum(jnp.concatenate(rows, axis=0), axis=1, keepdims=True)
    slot = lax.broadcasted_iota(I32, (LANES, slots), 1).astype(F32)
    return jnp.where(slot + 1.0 == index, 1.0, 0.0).astype(BF16)


def rows_of(ref, width, first, last):
    return jnp.concatenate([ref[:, q * width : (q + 1) * width] for q in range(first, last)], axis=0)


def picked(hot, field):
    hi, lo = halves(field)
    both = jnp.concatenate([hi, lo], axis=1).astype(BF16)
    hots = jnp.concatenate([hot, hot], axis=1)
    return lax.dot_general(hots, both, (((1,), (1,)), ((), ())), preferred_element_type=F32)


def pack(out_ref, plane, fine_ref, coarse_ref, send_fine_ref, send_coarse_ref):
    hot = picker(send_fine_ref, plane, LANES)
    out_ref[:, 0:256] = jnp.zeros((LANES, 256), F32)
    out_ref[:, 0 : NQ * BP] = picked(hot, rows_of(fine_ref, LANES, 0, NQ))
    hot = picker(send_coarse_ref, plane, 2 * LANES)
    low = picked(hot, rows_of(coarse_ref, 2 * LANES, 0, 5))
    high = picked(hot, rows_of(coarse_ref, 2 * LANES, 5, NQ))
    high = jnp.concatenate([high, jnp.zeros((LANES, BP), F32)], axis=1)
    s = lax.broadcasted_iota(I32, (LANES, 5 * BP), 0) & 7
    out_ref[:, 256:ROW] = jnp.zeros((LANES, LANES), F32)
    out_ref[:, 256 : 256 + 5 * BP] = jnp.where(s < 4, low, high)


def unpack(mine_ref, back_ref, prior, fine_ref, coarse_ref):
    parts = []
    for i in range(8):
        for rel in range(2):
            parts.append(mine_ref[i, rel, 0] + back_ref[i, 1 - rel])
    rows = jnp.concatenate(parts, axis=0)
    turned = [rows[:, t * LANES : (t + 1) * LANES].T for t in range(3)]
    fine = jnp.concatenate(turned[:2], axis=0)
    coarse = turned[2]
    for q in range(NQ):
        fine_ref[:, q * LANES : (q + 1) * LANES] = fine[q * BP : (q + 1) * BP]
        at = (q % 5) * BP
        coarse_ref[:, q * LANES : (q + 1) * LANES] = coarse[at : at + BP]


def first_kernel(
    fine_state, coarse_state, fine_star, coarse_star, send_fine, send_coarse, stiff,
    fine_flux, coarse_flux, neighbors, faces, turns, c_neighbors, c_faces, c_turns,
    stiff_volume, lift, project, rotate, count,
    keep, swap, x_fine, i_fine, x_coarse, c_first, c_second, star_f, star_c, send_f, send_c,
    flux_f, flux_c, nbr_f, face_f, turn_f, nbr_c, face_c, turn_c,
    w_time, w_vol, w_proj, w_rot, w_lift,
    state_f, state_c, stiff_v, vol_v, lift_v, project_v, rotate_v, lift_t,
    d_fine, t_fine, d_coarse, t_coarse, sems,
):
    moves = [
        (stiff, stiff_v), (fine_state, state_f), (fine_star, star_f), (coarse_state, state_c),
        (coarse_star, star_c), (send_fine, send_f), (send_coarse, send_c),
        (stiff_volume, vol_v), (lift, lift_v), (project, project_v), (rotate, rotate_v),
        (neighbors, nbr_f), (faces, face_f), (turns, turn_f),
        (c_neighbors, nbr_c), (c_faces, face_c), (c_turns, turn_c),
        (fine_flux, flux_f), (coarse_flux, flux_c),
    ]
    copies = [pltpu.make_async_copy(s, d, sems.at[i]) for i, (s, d) in enumerate(moves)]
    for copy in copies:
        copy.start()
    copies[0].wait()
    fill_weight(w_time, [stiff_v[d] for d in range(3)], BP, BP)
    w = weight(w_time, BP)

    def emit_coarse(tile, *terms):
        put(c_first, combine(FIRST_HALF, *terms), 2 * LANES, tile)
        put(c_second, combine(SECOND_HALF, *terms), 2 * LANES, tile)

    live = lax.broadcasted_iota(I32, (BP, LANES), 1) < count[0]

    def emit_fine(tile, *terms):
        values = combine(FIRST_HALF, *terms)
        put(i_fine, [jnp.where(live, v, 0.0) for v in values], LANES, tile)

    copies[1].wait()
    load_state(state_f, x_fine, LANES)
    copies[2].wait()
    predictor(x_fine, d_fine, t_fine, star_f, w, LANES, emit_fine)
    copies[3].wait()
    load_state(state_c, x_coarse, 2 * LANES)
    copies[4].wait()
    predictor(x_coarse, d_coarse, t_coarse, star_c, w, 2 * LANES, emit_coarse)
    for copy in copies[5:11]:
        copy.wait()
    fill_weight(w_vol, [vol_v[d] for d in range(3)], BP, BP)
    fill_weight(w_proj, [project_v[:, f, :] for f in range(4)], FP, BP)
    fill_weight(w_rot, [rotate_v[h] for h in range(3)], FP, FP)
    lift_t[...] = jnp.zeros(lift_t.shape, F32)
    for i in range(4):
        lift_t[i * FP : i * FP + FNB, 0:NB] = lift_v[:, i, :]
    hi, lo = halves(lift_t[...].T[0:BP, 0:32])
    w_lift[...] = jnp.zeros(w_lift.shape, F32)
    w_lift[:, 0:32] = hi
    w_lift[:, 32:64] = hi
    w_lift[:, 64:96] = lo
    core = place()[2]
    pack(swap, 1 - core, i_fine, c_first, send_f, send_c)
    pack(keep, core, i_fine, c_first, send_f, send_c)
    for copy in copies[11:]:
        copy.wait()


def locate(n):
    me, _, core = place()
    local = n < 384
    fine = n < 480
    g = jnp.where(fine, n - 384, n - 480)
    j = jnp.where(fine, g >> 3, g >> 2)
    s = jnp.where(fine, g & 7, g & 3)
    offset = j - REACH + jnp.where(j >= REACH, 1, 0)
    block = ((me - offset) & 15) ^ core
    lane = jnp.where(local, n & 127, block * 8 + s)
    tile = jnp.where(local, n >> 7, jnp.where(fine, 3, 4))
    return tile, lane


def correct(
    state_ref, i_ref, width, tables, neighbors, faces, turns, star_ref, flux_ref, weights,
    p_ref, t_ref, n_ref, l_ref, emit,
):
    w_vol, w_proj, w_rot, w_lift = weights
    p_ref[...] = mm(w_proj, i_ref[...])
    t_ref[...] = mm(w_vol, i_ref[...])
    for tile in range(width // LANES):
        lanes = slice(tile * LANES, (tile + 1) * LANES)
        for i in range(4):
            number = jnp.broadcast_to(neighbors[i : i + 1, lanes], (8, LANES))
            where_tile, lane = locate(number)
            later = jnp.where(where_tile == 4, lane + 4, lane)
            masks = [where_tile == k for k in range(5)]
            for q in range(NQ):
                at = lane if q < 5 else later
                for g in range(3):
                    value = None
                    for k, (ref, ref_width, ref_tile) in enumerate(tables):
                        start = q * ref_width + ref_tile * LANES
                        source = ref[8 * g : 8 * g + 8, start : start + LANES]
                        found = jnp.take_along_axis(source, at, axis=1)
                        value = found if value is None else jnp.where(masks[k], found, value)
                    n_ref[8 * g : 8 * g + 8, q * LANES : (q + 1) * LANES] = value
            projected = mm(w_proj, n_ref[...])
            face = jnp.broadcast_to(faces[i : i + 1, lanes], (FP, LANES))
            turn = jnp.broadcast_to(turns[i : i + 1, lanes], (FP, LANES))
            chosen = []
            for q in range(NQ):
                at = slice(q * LANES, (q + 1) * LANES)
                value = projected[0:FP, at]
                for f in range(1, 4):
                    value = jnp.where(face == f, projected[f * FP : (f + 1) * FP, at], value)
                chosen.append(value)
            rotated = mm(w_rot, jnp.concatenate(chosen, axis=1))
            acc = [None] * NQ
            for q in range(NQ):
                at = slice(q * LANES, (q + 1) * LANES)
                other = rotated[0:FP, at]
                for h in range(1, 3):
                    other = jnp.where(turn == h, rotated[h * FP : (h + 1) * FP, at], other)
                start = q * width + tile * LANES
                own = p_ref[i * FP : (i + 1) * FP, start : start + LANES]
                for p in range(NQ):
                    term = own * flux_ref[0, q, p, i : i + 1, lanes]
                    term = term + other * flux_ref[1, q, p, i : i + 1, lanes]
                    acc[p] = term if acc[p] is None else acc[p] + term
            for p in range(NQ):
                l_ref[i * FP : (i + 1) * FP, p * LANES : (p + 1) * LANES] = acc[p]
        lifted = mm(w_lift, l_ref[...])
        volume = star_sum(t_ref, star_ref, width, tile)
        state = get(state_ref, width, tile)
        emit(
            tile,
            [state[p] + (volume[p] + lifted[:, p * LANES : (p + 1) * LANES]) for p in range(NQ)],
        )


def second_kernel(
    mine, back, x_fine, i_fine, c_first, c_second, star_f, flux_f,
    neighbors, faces, turns, send_fine, send_coarse, w_time, w_vol, w_proj, w_rot, w_lift, count,
    keep, swap, x_next, i_next, ghost_f, ghost_c,
    p_ref, t_ref, n_ref, l_ref, d_ref,
):
    weights = weight(w_vol, BP), weight(w_proj, BP), weight(w_rot, FP), weight(w_lift, 32)
    unpack(mine, back, None, ghost_f, ghost_c)
    live = lax.broadcasted_iota(I32, (BP, LANES), 1) < count[0]
    tables = [
        (i_fine, LANES, 0), (c_first, 2 * LANES, 0), (c_first, 2 * LANES, 1),
        (ghost_f, LANES, 0), (ghost_c, LANES, 0),
    ]

    def emit_state(tile, values):
        old = get(x_fine, LANES, 0)
        put(x_next, [jnp.where(live, v, o) for v, o in zip(values, old)], LANES, 0)

    correct(
        x_fine, i_fine, LANES, tables, neighbors, faces, turns, star_f, flux_f, weights,
        p_ref, t_ref, n_ref, l_ref, emit_state,
    )

    def emit_fine(tile, *terms):
        values = combine(FIRST_HALF, *terms)
        put(i_next, [jnp.where(live, v, 0.0) for v in values], LANES, 0)

    predictor(x_next, d_ref, t_ref, star_f, weight(w_time, BP), LANES, emit_fine)
    core = place()[2]
    pack(swap, 1 - core, i_next, c_second, send_fine, send_coarse)
    pack(keep, core, i_next, c_second, send_fine, send_coarse)


def third_kernel(
    mine, back, x_fine, i_first, i_fine, x_coarse, c_first, c_second, g_fine, g_coarse,
    fine_star, fine_flux, coarse_star, coarse_flux,
    neighbors, faces, turns, c_neighbors, c_faces, c_turns, w_vol, w_proj, w_rot, w_lift, count,
    fine_out, coarse_out,
    p_ref, t_ref, n_ref, l_ref, pc_ref, tc_ref, ghost_f, ghost_c, c_full, i_both,
    fine_v, coarse_v, sems,
):
    weights = weight(w_vol, BP), weight(w_proj, BP), weight(w_rot, FP), weight(w_lift, 32)
    unpack(mine, back, None, ghost_f, ghost_c)
    live = lax.broadcasted_iota(I32, (NB, LANES), 1) < count[0]
    tables = [
        (i_fine, LANES, 0), (c_second, 2 * LANES, 0), (c_second, 2 * LANES, 1),
        (ghost_f, LANES, 0), (ghost_c, LANES, 0),
    ]

    def emit_fine(tile, values):
        old = get(x_fine, LANES, 0)
        for p in range(NQ):
            fine_v[p] = jnp.where(live, values[p][:NB], old[p][:NB])

    correct(
        x_fine, i_fine, LANES, tables, neighbors, faces, turns, fine_star, fine_flux, weights,
        p_ref, t_ref, n_ref, l_ref, emit_fine,
    )
    fine_copy = pltpu.make_async_copy(fine_v, fine_out, sems.at[0])
    fine_copy.start()
    c_full[...] = c_first[...] + c_second[...]
    i_both[...] = i_first[...] + i_fine[...]
    ghost_f[...] = ghost_f[...] + g_fine[...]
    ghost_c[...] = ghost_c[...] + g_coarse[...]
    tables = [
        (i_both, LANES, 0), (c_full, 2 * LANES, 0), (c_full, 2 * LANES, 1),
        (ghost_f, LANES, 0), (ghost_c, LANES, 0),
    ]

    def emit_coarse(tile, values):
        for p in range(NQ):
            coarse_v[p, :, tile * LANES : (tile + 1) * LANES] = values[p][:NB]

    correct(
        x_coarse, c_full, 2 * LANES, tables, c_neighbors, c_faces, c_turns, coarse_star,
        coarse_flux, weights, pc_ref, tc_ref, n_ref, l_ref, emit_coarse,
    )
    coarse_copy = pltpu.make_async_copy(coarse_v, coarse_out, sems.at[1])
    coarse_copy.start()
    fine_copy.wait()
    coarse_copy.wait()


VM = pl.BlockSpec(memory_space=pltpu.VMEM)
SM = pl.BlockSpec(memory_space=pltpu.SMEM)
ANY = pl.BlockSpec(memory_space=pltpu.HBM)

FINE = (BP, NQ * LANES)
COARSE = (BP, 2 * NQ * LANES)
FACES_F = (4 * FP, NQ * LANES)
FACES_C = (4 * FP, 2 * NQ * LANES)
STIFF_F = (3 * BP, NQ * LANES)
STIFF_C = (3 * BP, 2 * NQ * LANES)
SENT = (LANES, ROW)
WEIGHTS = [(3 * BP, LANES), (4 * FP, LANES), (3 * FP, LANES), (BP, LANES)]
PARAMS = pltpu.CompilerParams(vmem_limit_bytes=24 * 1024 * 1024)


def call(kernel, name, outs, scratches, args, count, hbm_in=False, hbm_out=False, sems=0, us=2):
    if hbm_in:
        args = [pltpu.with_memory_space_constraint(a, pltpu.HBM) for a in args]
    kinds = [pltpu.VMEM(s, F32) if isinstance(s, tuple) else s for s in scratches]
    if sems:
        kinds.append(pltpu.SemaphoreType.DMA((sems,)))
    return pl.pallas_call(
        kernel,
        name=name,
        in_specs=[ANY if hbm_in else VM] * len(args) + [SM] * len(count),
        out_specs=[ANY if hbm_out else VM] * len(outs),
        out_shape=[jax.ShapeDtypeStruct(s, F32) if isinstance(s, tuple) else s for s in outs],
        scratch_shapes=kinds,
        compiler_params=PARAMS,
        cost_estimate=pl.CostEstimate(flops=us * 10**9, bytes_accessed=us * 10**6, transcendentals=0),
    )(*args, *count)


def planes():
    groups = []
    for core in range(2):
        for k in range(8):
            first = [8 * k + i for i in range(8)]
            second = [(8 * k - 4 + (i + 4) % 8) % 64 for i in range(8)]
            groups.append([2 * chip + core for chip in (second if core else first)])
    return groups


SIBLING = [(i, i ^ 1) for i in range(N_DEV)]


def exchange(keep, swap):
    arrived = lax.ppermute(swap, "dom", SIBLING)
    blocks = jnp.stack([keep.reshape(8, 2, 8, ROW), arrived.reshape(8, 2, 8, ROW)], axis=1)
    got = lax.all_to_all(blocks, "dom", 0, 0, axis_index_groups=planes(), tiled=True)
    back = lax.ppermute(got[:, :, 1], "dom", SIBLING)
    return got, back


def local(
    fine_state, coarse_state, fine_star, coarse_star, fine_flux, coarse_flux,
    fine_neighbors, fine_faces, fine_turns, coarse_neighbors, coarse_faces, coarse_turns,
    fine_count, send_fine, send_coarse,
    stiff_time, stiff_volume, face_lift, face_project, face_rotate,
):
    fine_state, coarse_state = [s.transpose(1, 0, 2) for s in (fine_state, coarse_state)]
    fine_star, coarse_star = [s.transpose(1, 2, 0, 3) for s in (fine_star, coarse_star)]
    fine_flux, coarse_flux = [s.transpose(0, 2, 3, 1, 4) for s in (fine_flux, coarse_flux)]
    send_fine, send_coarse = [s.transpose(0, 2, 1) for s in (send_fine, send_coarse)]
    face_lift = face_lift.transpose(2, 0, 1)
    face_project = face_project.transpose(1, 0, 2)
    count = (fine_count,)
    links = (fine_neighbors, fine_faces, fine_turns, coarse_neighbors, coarse_faces, coarse_turns)
    fixed = (stiff_volume, face_lift, face_project, face_rotate)
    (keep, swap, x_fine, i_first, x_coarse, c_first, c_second, fine_star, coarse_star,
     send_fine, send_coarse, fine_flux, coarse_flux, *rest) = call(
        first_kernel, "predict",
        [SENT, SENT, FINE, FINE, COARSE, COARSE, COARSE, fine_star.shape, coarse_star.shape]
        + [jax.ShapeDtypeStruct(s.shape, I32) for s in (send_fine, send_coarse)]
        + [fine_flux.shape, coarse_flux.shape]
        + [jax.ShapeDtypeStruct(s.shape, I32) for s in links]
        + WEIGHTS[:1] + WEIGHTS,
        [fine_state.shape, coarse_state.shape, stiff_time.shape] + [f.shape for f in fixed]
        + [(LANES, LANES), FINE, STIFF_F, COARSE, STIFF_C],
        (fine_state, coarse_state, fine_star, coarse_star, send_fine, send_coarse, stiff_time,
         fine_flux, coarse_flux, *links, *fixed),
        count, hbm_in=True, sems=19,
    )
    links, (w_time, *weights) = rest[:6], rest[6:]
    mine, back = exchange(keep, swap)
    keep, swap, x_next, i_second, g_fine, g_coarse = call(
        second_kernel, "substep",
        [SENT, SENT, FINE, FINE, FINE, FINE],
        [FACES_F, STIFF_F, FINE, FACES_F, FINE],
        (mine, back, x_fine, i_first, c_first, c_second, fine_star, fine_flux, *links[:3],
         send_fine, send_coarse, w_time, *weights), count,
    )
    mine, back = exchange(keep, swap)
    results = call(
        third_kernel, "finish",
        [(NQ, NB, LANES), (NQ, NB, 2 * LANES)],
        [FACES_F, STIFF_F, FINE, FACES_F, FACES_C, STIFF_C, FINE, FINE, COARSE, FINE,
         (NQ, NB, LANES), (NQ, NB, 2 * LANES)],
        (mine, back, x_next, i_first, i_second, x_coarse, c_first, c_second, g_fine, g_coarse,
         fine_star, fine_flux, coarse_star, coarse_flux, *links, *weights), count,
        hbm_out=True, sems=2,
    )
    return tuple(r.transpose(1, 0, 2) for r in results)


def solution(mesh):
    placed = (
        P(None, None, "dom"),
        P(None, None, "dom"),
        P(None, None, None, "dom"),
        P(None, None, None, "dom"),
        P(None, None, None, None, "dom"),
        P(None, None, None, None, "dom"),
        P(None, "dom"),
        P(None, "dom"),
        P(None, "dom"),
        P(None, "dom"),
        P(None, "dom"),
        P(None, "dom"),
        P("dom"),
        P("dom", None, None),
        P("dom", None, None),
        P(),
        P(),
        P(),
        P(),
        P(),
    )
    return jax.shard_map(
        local,
        mesh=mesh,
        in_specs=placed,
        out_specs=(P(None, None, "dom"), P(None, None, "dom")),
        check_vma=False,
    )
```

```python
from functools import partial

import jax
import jax.numpy as jnp
from jax import lax
from jax.experimental import pallas as pl
from jax.experimental.pallas import tpu as pltpu
from jax.sharding import PartitionSpec as P

NB = 20
NQ = 9
FNB = 6
REACH = 6
BP = 24
FP = 8
LANES = 128
ROW = 384
FIRST_HALF = (0.5, 0.125, 1.0 / 48.0)
SECOND_HALF = (0.5, 0.375, 7.0 / 48.0)
F32 = jnp.float32
BF16 = jnp.bfloat16
I32 = jnp.int32
N_DEV = 128
BLOCKS = 13
KEPT = 48


def halves(x):
    hi = x.astype(BF16).astype(F32)
    return hi, x - hi


def stacked(x):
    hi, lo = halves(x)
    return jnp.concatenate([hi, lo, hi], axis=0).astype(BF16)


def fill_weight(ref, blocks, row_step, col_step):
    ref[...] = jnp.zeros(ref.shape, F32)
    for i, block in enumerate(blocks):
        rows, cols = block.shape
        hi, lo = halves(block)
        span = slice(i * row_step, i * row_step + rows)
        ref[span, 0:cols] = hi
        ref[span, col_step : col_step + cols] = hi
        ref[span, 2 * col_step : 2 * col_step + cols] = lo


def weight(ref, depth):
    return ref[:, 0 : 3 * depth].astype(BF16)


def mm(w, x):
    return jnp.dot(w, stacked(x), preferred_element_type=F32)


def load_state(state_ref, x_ref, width):
    for q in range(NQ):
        x_ref[NB:BP, q * width : (q + 1) * width] = jnp.zeros((BP - NB, width), F32)
        x_ref[0:NB, q * width : (q + 1) * width] = state_ref[q]


def star_sum(t_ref, star_ref, width, tile):
    lanes = slice(tile * LANES, (tile + 1) * LANES)
    acc = [None] * NQ
    for q in range(NQ):
        for d in range(3):
            t = t_ref[d * BP : (d + 1) * BP, q * width + tile * LANES : q * width + (tile + 1) * LANES]
            for p in range(NQ):
                term = t * star_ref[q, p, d : d + 1, lanes]
                acc[p] = term if acc[p] is None else acc[p] + term
    return acc


def put(ref, values, width, tile):
    for p in range(NQ):
        ref[:, p * width + tile * LANES : p * width + (tile + 1) * LANES] = values[p]


def get(ref, width, tile):
    return [
        ref[:, p * width + tile * LANES : p * width + (tile + 1) * LANES] for p in range(NQ)
    ]


def first_term(x_ref, d_ref, t_ref, star_ref, width):
    for tile in range(width // LANES):
        put(d_ref, star_sum(t_ref, star_ref, width, tile), width, tile)


def second_term(x_ref, d_ref, t_ref, star_ref, width, emit):
    for tile in range(width // LANES):
        second = star_sum(t_ref, star_ref, width, tile)
        emit(tile, get(x_ref, width, tile), get(d_ref, width, tile), second)


def combine(weights, state, neg_first, second):
    return [
        weights[0] * s - weights[1] * f + weights[2] * g
        for s, f, g in zip(state, neg_first, second)
    ]


def place():
    me = lax.axis_index("dom").astype(I32)
    return me, me >> 1, me & 1


def route(block):
    me, chip, core = place()
    if block == 12:
        offset = 1 - 2 * core
    else:
        sender = core if block < 6 else 1 - core
        ahead = 1 - 2 * sender
        distance = (block % 6) // 2 + 1
        offset = 2 * ahead * distance + (sender ^ (block % 2)) - core
    target = me + offset
    valid = (target >= 0) & (target < N_DEV) & (offset >= -REACH) & (offset <= REACH)
    peer = jnp.where(offset < 0, offset + REACH, offset + REACH - 1)
    return jnp.where(valid, peer, -1)


def picker(send_ref, slots):
    table = send_ref[0].astype(F32) + 1.0
    if table.shape[0] < 8:
        table = jnp.concatenate([table, table], axis=0)
    lane = lax.broadcasted_iota(I32, table.shape, 1)
    rows = []
    for block in range(BLOCKS):
        rows.append(jnp.where(lane == route(block), table, 0.0))
    index = jnp.sum(jnp.concatenate(rows, axis=0), axis=1, keepdims=True)
    slot = lax.broadcasted_iota(I32, (BLOCKS * 8, slots), 1).astype(F32)
    return jnp.where(slot + 1.0 == index, 1.0, 0.0).astype(BF16)


def rows_of(ref, width, first, last):
    return jnp.concatenate([ref[:, q * width : (q + 1) * width] for q in range(first, last)], axis=0)


def picked(hot, field):
    hi, lo = halves(field)
    both = jnp.concatenate([hi, lo], axis=1).astype(BF16)
    hots = jnp.concatenate([hot, hot], axis=1)
    return lax.dot_general(hots, both, (((1,), (1,)), ((), ())), preferred_element_type=F32)


def pack(keep_ref, swap_ref, fine_ref, coarse_ref, send_fine_ref, send_coarse_ref):
    fine = picked(picker(send_fine_ref, LANES), rows_of(fine_ref, LANES, 0, NQ))
    hot = picker(send_coarse_ref, 2 * LANES)
    low = picked(hot, rows_of(coarse_ref, 2 * LANES, 0, 5))
    high = picked(hot, rows_of(coarse_ref, 2 * LANES, 5, NQ))
    high = jnp.concatenate([high, jnp.zeros((BLOCKS * 8, BP), F32)], axis=1)
    s = lax.broadcasted_iota(I32, (BLOCKS * 8, 5 * BP), 0) & 7
    coarse = jnp.where(s < 4, low, high)
    for ref, rows in ((keep_ref, slice(0, KEPT)), (swap_ref, slice(KEPT, BLOCKS * 8))):
        ref[:, 128:ROW] = jnp.zeros((ref.shape[0], ROW - LANES), F32)
        ref[:, 0 : NQ * BP] = fine[rows]
        ref[:, 256 : 256 + 5 * BP] = coarse[rows]


def unpack(arrived, fine_ref, coarse_ref):
    *direct, back, sibling = arrived
    parts = []
    for ref in direct:
        parts += [ref[0:8], ref[16:24]]
    parts += [back[...], sibling[KEPT : KEPT + 8], jnp.zeros((LANES - BLOCKS * 8, ROW), F32)]
    rows = jnp.concatenate(parts, axis=0)
    turned = [rows[:, t * LANES : (t + 1) * LANES].T for t in range(3)]
    fine = jnp.concatenate(turned[:2], axis=0)
    for q in range(NQ):
        fine_ref[:, q * LANES : (q + 1) * LANES] = fine[q * BP : (q + 1) * BP]
    for q in range(5):
        coarse_ref[:, q * LANES : (q + 1) * LANES] = turned[2][q * BP : (q + 1) * BP]


def first_kernel(
    fine_state, coarse_state, fine_star, coarse_star, send_fine, send_coarse, stiff,
    fine_flux, coarse_flux, neighbors, faces, turns, c_neighbors, c_faces, c_turns,
    stiff_volume, lift, project, rotate, count,
    keep, swap, x_fine, i_fine, x_coarse, c_first, c_second, star_f, star_c, send_f, send_c,
    flux_f, flux_c, nbr_f, face_f, turn_f, nbr_c, face_c, turn_c,
    w_time, w_vol, w_proj, w_rot, w_lift,
    state_f, state_c, stiff_v, vol_v, lift_v, project_v, rotate_v, lift_t,
    d_fine, t_fine, d_coarse, t_coarse, sems,
):
    moves = [
        (stiff, stiff_v), (fine_state, state_f), (fine_star, star_f), (coarse_state, state_c),
        (coarse_star, star_c), (send_fine, send_f), (send_coarse, send_c),
        (stiff_volume, vol_v), (lift, lift_v), (project, project_v), (rotate, rotate_v),
        (neighbors, nbr_f), (faces, face_f), (turns, turn_f),
        (c_neighbors, nbr_c), (c_faces, face_c), (c_turns, turn_c),
        (fine_flux, flux_f), (coarse_flux, flux_c),
    ]
    copies = [pltpu.make_async_copy(s, d, sems.at[i]) for i, (s, d) in enumerate(moves)]
    for copy in copies:
        copy.start()
    copies[0].wait()
    fill_weight(w_time, [stiff_v[d] for d in range(3)], BP, BP)
    w = weight(w_time, BP)

    def emit_coarse(tile, *terms):
        put(c_first, combine(FIRST_HALF, *terms), 2 * LANES, tile)
        put(c_second, combine(SECOND_HALF, *terms), 2 * LANES, tile)

    live = lax.broadcasted_iota(I32, (BP, LANES), 1) < count[0]

    def emit_fine(tile, *terms):
        values = combine(FIRST_HALF, *terms)
        put(i_fine, [jnp.where(live, v, 0.0) for v in values], LANES, tile)

    copies[1].wait()
    load_state(state_f, x_fine, LANES)
    t_fine[...] = mm(w, x_fine[...])
    copies[3].wait()
    load_state(state_c, x_coarse, 2 * LANES)
    t_coarse[...] = mm(w, x_coarse[...])
    copies[2].wait()
    first_term(x_fine, d_fine, t_fine, star_f, LANES)
    t_fine[...] = mm(w, d_fine[...])
    copies[4].wait()
    first_term(x_coarse, d_coarse, t_coarse, star_c, 2 * LANES)
    t_coarse[...] = mm(w, d_coarse[...])
    second_term(x_fine, d_fine, t_fine, star_f, LANES, emit_fine)
    second_term(x_coarse, d_coarse, t_coarse, star_c, 2 * LANES, emit_coarse)
    for copy in copies[5:11]:
        copy.wait()
    fill_weight(w_vol, [vol_v[d] for d in range(3)], BP, BP)
    fill_weight(w_proj, [project_v[:, f, :] for f in range(4)], FP, BP)
    w_rot[...] = jnp.zeros(w_rot.shape, F32)
    for h in range(3):
        w_rot[h * FP : h * FP + FNB, 0:FNB] = rotate_v[h]
    lift_t[...] = jnp.zeros(lift_t.shape, F32)
    for i in range(4):
        lift_t[i * FP : i * FP + FNB, 0:NB] = lift_v[:, i, :]
    hi, lo = halves(lift_t[...].T[0:BP, 0:32])
    w_lift[...] = jnp.zeros(w_lift.shape, F32)
    w_lift[:, 0:32] = hi
    w_lift[:, 32:64] = hi
    w_lift[:, 64:96] = lo
    pack(keep, swap, i_fine, c_first, send_f, send_c)
    for copy in copies[11:]:
        copy.wait()


def locate(n):
    me, chip, core = place()
    local = n < 384
    fine = n < 480
    g = jnp.where(fine, n - 384, n - 480)
    j = jnp.where(fine, g >> 3, g >> 2)
    s = jnp.where(fine, g & 7, g & 3)
    offset = j - REACH + jnp.where(j >= REACH, 1, 0)
    source = me - offset
    away = (source >> 1) - chip
    apart = jnp.abs(away)
    ahead = 1 - 2 * core
    direct = away * ahead < 0
    other = (source & 1) ^ core
    block = 2 * (apart - 1) + jnp.where(direct, other, 7 - other)
    block = jnp.where(away == 0, 12, block)
    lane = jnp.where(local, n & 127, block * 8 + s)
    tile = jnp.where(local, n >> 7, jnp.where(fine, 3, 4))
    return tile, lane


def spread(row_ref, i, tile):
    return jnp.broadcast_to(row_ref[i : i + 1, tile * LANES : (tile + 1) * LANES], (8, LANES))


def pick(options, bits):
    if len(options) == 1:
        return options[0]
    pairs = [options[i : i + 2] for i in range(0, len(options), 2)]
    merged = [jnp.where(bits[0], p[1], p[0]) if len(p) == 2 else p[0] for p in pairs]
    return pick(merged, bits[1:])


def bits_of(number, count):
    return [(number & (1 << k)) != 0 for k in range(count)]


def correct(
    state_ref, width, own_ref, tables, neighbors, faces, turns, star_ref, flux_ref, w_rot, w_lift,
    t_ref, n_ref, l_ref, emit,
):
    turned = [
        [jnp.broadcast_to(w_rot[h * FP : (h + 1) * FP, b : b + 1], (FP, LANES)) for h in range(3)]
        for b in range(FNB)
    ]
    for tile in range(width // LANES):
        lanes = slice(tile * LANES, (tile + 1) * LANES)
        for i in range(4):
            kind, lane = locate(spread(neighbors, i, tile))
            later = jnp.where(kind == 4, lane + 4, lane)
            face = spread(faces, i, tile)
            turn = spread(turns, i, tile)
            kinds = bits_of(kind, 3)
            numbers = bits_of(face, 2)
            for q in range(NQ):
                at = lane if q < 5 else later
                found = []
                for k, (ref, ref_width, ref_tile) in enumerate(tables):
                    start = (q if k < 4 else q % 5) * ref_width + ref_tile * LANES
                    found.append(pick([
                        jnp.take_along_axis(
                            ref[f * FP : (f + 1) * FP, start : start + LANES], at, axis=1
                        )
                        for f in range(4)
                    ], numbers))
                n_ref[i, :, q * LANES : (q + 1) * LANES] = pick(found, kinds)
            turn_by = [pick(turned[b], bits_of(turn, 2)) for b in range(FNB)]
            acc = [None] * NQ
            for q in range(NQ):
                at = slice(q * LANES, (q + 1) * LANES)
                other = turn_by[0] * n_ref[i, 0:1, at]
                for b in range(1, FNB):
                    other = other + turn_by[b] * n_ref[i, b : b + 1, at]
                start = q * width + tile * LANES
                own = own_ref[i * FP : (i + 1) * FP, start : start + LANES]
                for p in range(NQ):
                    term = own * flux_ref[0, q, p, i : i + 1, lanes]
                    term = term + other * flux_ref[1, q, p, i : i + 1, lanes]
                    acc[p] = term if acc[p] is None else acc[p] + term
            for p in range(NQ):
                l_ref[i * FP : (i + 1) * FP, p * LANES : (p + 1) * LANES] = acc[p]
        lifted = mm(w_lift, l_ref[...])
        volume = star_sum(t_ref, star_ref, width, tile)
        state = get(state_ref, width, tile)
        emit(
            tile,
            [state[p] + (volume[p] + lifted[:, p * LANES : (p + 1) * LANES]) for p in range(NQ)],
        )


def second_kernel(
    got_1, got_2, got_3, back, sibling, x_fine, i_fine, c_first, c_second, star_f, flux_f,
    neighbors, faces, turns, send_fine, send_coarse, w_time, w_vol, w_proj, w_rot, w_lift, count,
    keep, swap, x_next, i_next, p_own, p_coarse, p_gf, p_gc,
    ghost_f, ghost_c, t_ref, n_ref, l_ref, d_ref,
):
    w_v, w_p = weight(w_vol, BP), weight(w_proj, BP)
    t_ref[...] = mm(w_v, i_fine[...])
    p_own[...] = mm(w_p, i_fine[...])
    p_coarse[...] = mm(w_p, c_first[...])
    unpack((got_1, got_2, got_3, back, sibling), ghost_f, ghost_c)
    p_gf[...] = mm(w_p, ghost_f[...])
    p_gc[...] = mm(w_p, ghost_c[...])
    live = lax.broadcasted_iota(I32, (BP, LANES), 1) < count[0]
    tables = [
        (p_own, LANES, 0), (p_coarse, 2 * LANES, 0), (p_coarse, 2 * LANES, 1),
        (p_gf, LANES, 0), (p_gc, LANES, 0),
    ]

    def emit_state(tile, values):
        old = get(x_fine, LANES, 0)
        put(x_next, [jnp.where(live, v, o) for v, o in zip(values, old)], LANES, 0)

    correct(
        x_fine, LANES, p_own, tables, neighbors, faces, turns, star_f, flux_f,
        w_rot, weight(w_lift, 32), t_ref, n_ref, l_ref, emit_state,
    )

    def emit_fine(tile, *terms):
        values = combine(FIRST_HALF, *terms)
        put(i_next, [jnp.where(live, v, 0.0) for v in values], LANES, 0)

    w = weight(w_time, BP)
    t_ref[...] = mm(w, x_next[...])
    first_term(x_next, d_ref, t_ref, star_f, LANES)
    t_ref[...] = mm(w, d_ref[...])
    second_term(x_next, d_ref, t_ref, star_f, LANES, emit_fine)
    pack(keep, swap, i_next, c_second, send_fine, send_coarse)


def third_kernel(
    got_1, got_2, got_3, back, sibling, x_fine, i_fine, x_coarse, c_first, c_second, p_own, p_coarse, p_gf, p_gc,
    fine_star, fine_flux, coarse_star, coarse_flux,
    neighbors, faces, turns, c_neighbors, c_faces, c_turns, w_vol, w_proj, w_rot, w_lift, count,
    fine_out, coarse_out,
    q_own, q_coarse, q_gf, q_gc, ghost_f, ghost_c, t_ref, tc_ref, n_ref, l_ref,
    fine_v, coarse_v, sems,
):
    w_v, w_p, w_l = weight(w_vol, BP), weight(w_proj, BP), weight(w_lift, 32)
    t_ref[...] = mm(w_v, i_fine[...])
    q_own[...] = mm(w_p, i_fine[...])
    q_coarse[...] = mm(w_p, c_second[...])
    tc_ref[...] = mm(w_v, c_first[...] + c_second[...])
    unpack((got_1, got_2, got_3, back, sibling), ghost_f, ghost_c)
    q_gf[...] = mm(w_p, ghost_f[...])
    q_gc[...] = mm(w_p, ghost_c[...])
    live = lax.broadcasted_iota(I32, (NB, LANES), 1) < count[0]
    tables = [
        (q_own, LANES, 0), (q_coarse, 2 * LANES, 0), (q_coarse, 2 * LANES, 1),
        (q_gf, LANES, 0), (q_gc, LANES, 0),
    ]

    def emit_fine(tile, values):
        old = get(x_fine, LANES, 0)
        for p in range(NQ):
            fine_v[p] = jnp.where(live, values[p][:NB], old[p][:NB])

    correct(
        x_fine, LANES, q_own, tables, neighbors, faces, turns, fine_star, fine_flux,
        w_rot, w_l, t_ref, n_ref, l_ref, emit_fine,
    )
    fine_copy = pltpu.make_async_copy(fine_v, fine_out, sems.at[0])
    fine_copy.start()
    for total, prior in ((q_own, p_own), (q_coarse, p_coarse), (q_gf, p_gf), (q_gc, p_gc)):
        total[...] = total[...] + prior[...]

    def emit_coarse(tile, values):
        for p in range(NQ):
            coarse_v[p, :, tile * LANES : (tile + 1) * LANES] = values[p][:NB]

    correct(
        x_coarse, 2 * LANES, q_coarse, tables, c_neighbors, c_faces, c_turns, coarse_star,
        coarse_flux, w_rot, w_l, tc_ref, n_ref, l_ref, emit_coarse,
    )
    coarse_copy = pltpu.make_async_copy(coarse_v, coarse_out, sems.at[1])
    coarse_copy.start()
    fine_copy.wait()
    coarse_copy.wait()


VM = pl.BlockSpec(memory_space=pltpu.VMEM)
SM = pl.BlockSpec(memory_space=pltpu.SMEM)
ANY = pl.BlockSpec(memory_space=pltpu.HBM)

FINE = (BP, NQ * LANES)
COARSE = (BP, 2 * NQ * LANES)
FACES_F = (4 * FP, NQ * LANES)
FACES_C = (4 * FP, 2 * NQ * LANES)
STIFF_F = (3 * BP, NQ * LANES)
STIFF_C = (3 * BP, 2 * NQ * LANES)
GHOST_C = (BP, 5 * LANES)
FACES_G = (4 * FP, 5 * LANES)
PICKED = (4, FP, NQ * LANES)
WEIGHTS = [(3 * BP, LANES), (4 * FP, LANES), (3 * FP, LANES), (BP, LANES)]
PARAMS = pltpu.CompilerParams(vmem_limit_bytes=24 * 1024 * 1024)


def call(kernel, name, outs, scratches, args, count, hbm_in=False, hbm_out=False, sems=0, us=2):
    if hbm_in:
        args = [pltpu.with_memory_space_constraint(a, pltpu.HBM) for a in args]
    kinds = [pltpu.VMEM(s, F32) if isinstance(s, tuple) else s for s in scratches]
    if sems:
        kinds.append(pltpu.SemaphoreType.DMA((sems,)))
    return pl.pallas_call(
        kernel,
        name=name,
        in_specs=[ANY if hbm_in else VM] * len(args) + [SM] * len(count),
        out_specs=[ANY if hbm_out else VM] * len(outs),
        out_shape=[jax.ShapeDtypeStruct(s, F32) if isinstance(s, tuple) else s for s in outs],
        scratch_shapes=kinds,
        compiler_params=PARAMS,
        cost_estimate=pl.CostEstimate(flops=us * 10**9, bytes_accessed=us * 10**6, transcendentals=0),
    )(*args, *count)


SIBLING = [(i, i ^ 1) for i in range(N_DEV)]


def ahead_by(distance):
    step = 2 * distance
    return [(i, (i + (step if i % 2 == 0 else -step)) % N_DEV) for i in range(N_DEV)]


def exchange(keep, swap):
    sibling = lax.ppermute(swap, "dom", SIBLING)
    sent = [jnp.concatenate([keep[16 * d : 16 * d + 16], sibling[16 * d : 16 * d + 16]]) for d in range(3)]
    got = [None] * 3
    for d in (2, 1, 0):
        got[d] = lax.ppermute(sent[d], "dom", ahead_by(d + 1))
    rest = [g.reshape(2, 2, 8, ROW)[:, 1].reshape(16, ROW) for g in got]
    back = lax.ppermute(jnp.concatenate(rest), "dom", SIBLING)
    return *got, back, sibling


def local(
    fine_state, coarse_state, fine_star, coarse_star, fine_flux, coarse_flux,
    fine_neighbors, fine_faces, fine_turns, coarse_neighbors, coarse_faces, coarse_turns,
    fine_count, send_fine, send_coarse,
    stiff_time, stiff_volume, face_lift, face_project, face_rotate,
):
    fine_state, coarse_state = [s.transpose(1, 0, 2) for s in (fine_state, coarse_state)]
    fine_star, coarse_star = [s.transpose(1, 2, 0, 3) for s in (fine_star, coarse_star)]
    fine_flux, coarse_flux = [s.transpose(0, 2, 3, 1, 4) for s in (fine_flux, coarse_flux)]
    send_fine, send_coarse = [s.transpose(0, 2, 1) for s in (send_fine, send_coarse)]
    face_lift = face_lift.transpose(2, 0, 1)
    face_project = face_project.transpose(1, 0, 2)
    count = (fine_count,)
    links = (fine_neighbors, fine_faces, fine_turns, coarse_neighbors, coarse_faces, coarse_turns)
    fixed = (stiff_volume, face_lift, face_project, face_rotate)
    (keep, swap, x_fine, i_first, x_coarse, c_first, c_second, fine_star, coarse_star,
     send_fine, send_coarse, fine_flux, coarse_flux, *rest) = call(
        first_kernel, "predict",
        [(KEPT, ROW), (KEPT + 8, ROW), FINE, FINE, COARSE, COARSE, COARSE, fine_star.shape, coarse_star.shape]
        + [jax.ShapeDtypeStruct(s.shape, I32) for s in (send_fine, send_coarse)]
        + [fine_flux.shape, coarse_flux.shape]
        + [jax.ShapeDtypeStruct(s.shape, I32) for s in links]
        + WEIGHTS[:1] + WEIGHTS,
        [fine_state.shape, coarse_state.shape, stiff_time.shape] + [f.shape for f in fixed]
        + [(LANES, LANES), FINE, STIFF_F, COARSE, STIFF_C],
        (fine_state, coarse_state, fine_star, coarse_star, send_fine, send_coarse, stiff_time,
         fine_flux, coarse_flux, *links, *fixed),
        count, hbm_in=True, sems=19,
    )
    links, (w_time, *weights) = rest[:6], rest[6:]
    arrived = exchange(keep, swap)
    keep, swap, x_next, i_second, *tables = call(
        second_kernel, "substep",
        [(KEPT, ROW), (KEPT + 8, ROW), FINE, FINE, FACES_F, FACES_C, FACES_F, FACES_G],
        [FINE, GHOST_C, STIFF_F, PICKED, FACES_F, FINE],
        (*arrived, x_fine, i_first, c_first, c_second, fine_star, fine_flux, *links[:3],
         send_fine, send_coarse, w_time, *weights), count,
    )
    arrived = exchange(keep, swap)
    results = call(
        third_kernel, "finish",
        [(NQ, NB, LANES), (NQ, NB, 2 * LANES)],
        [FACES_F, FACES_C, FACES_F, FACES_G, FINE, GHOST_C, STIFF_F, STIFF_C, PICKED, FACES_F,
         (NQ, NB, LANES), (NQ, NB, 2 * LANES)],
        (*arrived, x_next, i_second, x_coarse, c_first, c_second, *tables,
         fine_star, fine_flux, coarse_star, coarse_flux, *links, *weights), count,
        hbm_out=True, sems=2,
    )
    return tuple(r.transpose(1, 0, 2) for r in results)


def solution(mesh):
    placed = (
        P(None, None, "dom"),
        P(None, None, "dom"),
        P(None, None, None, "dom"),
        P(None, None, None, "dom"),
        P(None, None, None, None, "dom"),
        P(None, None, None, None, "dom"),
        P(None, "dom"),
        P(None, "dom"),
        P(None, "dom"),
        P(None, "dom"),
        P(None, "dom"),
        P(None, "dom"),
        P("dom"),
        P("dom", None, None),
        P("dom", None, None),
        P(),
        P(),
        P(),
        P(),
        P(),
    )
    return jax.shard_map(
        local,
        mesh=mesh,
        in_specs=placed,
        out_specs=(P(None, None, "dom"), P(None, None, "dom")),
        check_vma=False,
    )
```

```python
from functools import partial

import jax
import jax.numpy as jnp
from jax import lax
from jax.experimental import pallas as pl
from jax.experimental.pallas import tpu as pltpu
from jax.sharding import PartitionSpec as P

NB = 20
NQ = 9
FNB = 6
REACH = 6
BP = 24
FP = 8
LANES = 128
ROW = 384
FIRST_HALF = (0.5, 0.125, 1.0 / 48.0)
SECOND_HALF = (0.5, 0.375, 7.0 / 48.0)
F32 = jnp.float32
BF16 = jnp.bfloat16
I32 = jnp.int32
N_DEV = 128
BLOCKS = 13
KEPT = 48


def halves(x):
    hi = x.astype(BF16).astype(F32)
    return hi, x - hi


def stacked(x):
    hi, lo = halves(x)
    return jnp.concatenate([hi, lo, hi], axis=0).astype(BF16)


def fill_weight(ref, blocks, row_step, col_step):
    ref[...] = jnp.zeros(ref.shape, F32)
    for i, block in enumerate(blocks):
        rows, cols = block.shape
        hi, lo = halves(block)
        span = slice(i * row_step, i * row_step + rows)
        ref[span, 0:cols] = hi
        ref[span, col_step : col_step + cols] = hi
        ref[span, 2 * col_step : 2 * col_step + cols] = lo


def weight(ref, depth):
    return ref[:, 0 : 3 * depth].astype(BF16)


def mm(w, x):
    return jnp.dot(w, stacked(x), preferred_element_type=F32)


def load_state(state_ref, x_ref, width):
    for q in range(NQ):
        x_ref[NB:BP, q * width : (q + 1) * width] = jnp.zeros((BP - NB, width), F32)
        x_ref[0:NB, q * width : (q + 1) * width] = state_ref[q]


def star_sum(t_ref, star_ref, width, tile):
    lanes = slice(tile * LANES, (tile + 1) * LANES)
    acc = [None] * NQ
    for q in range(NQ):
        for d in range(3):
            t = t_ref[d * BP : (d + 1) * BP, q * width + tile * LANES : q * width + (tile + 1) * LANES]
            for p in range(NQ):
                term = t * star_ref[q, p, d : d + 1, lanes]
                acc[p] = term if acc[p] is None else acc[p] + term
    return acc


def put(ref, values, width, tile):
    for p in range(NQ):
        ref[:, p * width + tile * LANES : p * width + (tile + 1) * LANES] = values[p]


def get(ref, width, tile):
    return [
        ref[:, p * width + tile * LANES : p * width + (tile + 1) * LANES] for p in range(NQ)
    ]


def first_term(x_ref, d_ref, t_ref, star_ref, width):
    for tile in range(width // LANES):
        put(d_ref, star_sum(t_ref, star_ref, width, tile), width, tile)


def second_term(x_ref, d_ref, t_ref, star_ref, width, emit):
    for tile in range(width // LANES):
        second = star_sum(t_ref, star_ref, width, tile)
        emit(tile, get(x_ref, width, tile), get(d_ref, width, tile), second)


def combine(weights, state, neg_first, second):
    return [
        weights[0] * s - weights[1] * f + weights[2] * g
        for s, f, g in zip(state, neg_first, second)
    ]


def place():
    me = lax.axis_index("dom").astype(I32)
    return me, me >> 1, me & 1


def route(block):
    me, chip, core = place()
    if block == 12:
        offset = 1 - 2 * core
    else:
        sender = core if block < 6 else 1 - core
        ahead = 1 - 2 * sender
        distance = (block % 6) // 2 + 1
        offset = 2 * ahead * distance + (sender ^ (block % 2)) - core
    target = me + offset
    valid = (target >= 0) & (target < N_DEV) & (offset >= -REACH) & (offset <= REACH)
    peer = jnp.where(offset < 0, offset + REACH, offset + REACH - 1)
    return jnp.where(valid, peer, -1)


def picker(send_ref, slots):
    table = send_ref[0].astype(F32) + 1.0
    if table.shape[0] < 8:
        table = jnp.concatenate([table, table], axis=0)
    lane = lax.broadcasted_iota(I32, table.shape, 1)
    rows = []
    for block in range(BLOCKS):
        rows.append(jnp.where(lane == route(block), table, 0.0))
    index = jnp.sum(jnp.concatenate(rows, axis=0), axis=1, keepdims=True)
    slot = lax.broadcasted_iota(I32, (BLOCKS * 8, slots), 1).astype(F32)
    return jnp.where(slot + 1.0 == index, 1.0, 0.0).astype(BF16)


def rows_of(ref, width, first, last):
    return jnp.concatenate([ref[:, q * width : (q + 1) * width] for q in range(first, last)], axis=0)


def picked(hot, field):
    hi, lo = halves(field)
    both = jnp.concatenate([hi, lo], axis=1).astype(BF16)
    hots = jnp.concatenate([hot, hot], axis=1)
    return lax.dot_general(hots, both, (((1,), (1,)), ((), ())), preferred_element_type=F32)


def pack(keep_ref, swap_ref, fine_ref, coarse_ref, send_fine_ref, send_coarse_ref):
    fine = picked(picker(send_fine_ref, LANES), rows_of(fine_ref, LANES, 0, NQ))
    hot = picker(send_coarse_ref, 2 * LANES)
    low = picked(hot, rows_of(coarse_ref, 2 * LANES, 0, 5))
    high = picked(hot, rows_of(coarse_ref, 2 * LANES, 5, NQ))
    high = jnp.concatenate([high, jnp.zeros((BLOCKS * 8, BP), F32)], axis=1)
    s = lax.broadcasted_iota(I32, (BLOCKS * 8, 5 * BP), 0) & 7
    coarse = jnp.where(s < 4, low, high)
    for ref, rows in ((keep_ref, slice(0, KEPT)), (swap_ref, slice(KEPT, BLOCKS * 8))):
        ref[:, 128:ROW] = jnp.zeros((ref.shape[0], ROW - LANES), F32)
        ref[:, 0 : NQ * BP] = fine[rows]
        ref[:, 256 : 256 + 5 * BP] = coarse[rows]


def unpack(arrived, fine_ref, coarse_ref):
    *direct, back, sibling = arrived
    parts = []
    for ref in direct:
        parts += [ref[0:8], ref[16:24]]
    parts += [back[0:KEPT], sibling[KEPT : KEPT + 8], jnp.zeros((LANES - BLOCKS * 8, ROW), F32)]
    rows = jnp.concatenate(parts, axis=0)
    turned = [rows[:, t * LANES : (t + 1) * LANES].T for t in range(3)]
    fine = jnp.concatenate(turned[:2], axis=0)
    for q in range(NQ):
        fine_ref[:, q * LANES : (q + 1) * LANES] = fine[q * BP : (q + 1) * BP]
    for q in range(5):
        coarse_ref[:, q * LANES : (q + 1) * LANES] = turned[2][q * BP : (q + 1) * BP]


def first_kernel(
    fine_state, coarse_state, fine_star, coarse_star, send_fine, send_coarse, stiff,
    fine_flux, coarse_flux, neighbors, faces, turns, c_neighbors, c_faces, c_turns,
    stiff_volume, lift, project, rotate, count,
    keep, swap, x_fine, i_fine, x_coarse, c_first, c_second, star_f, star_c, send_f, send_c,
    flux_f, flux_c, nbr_f, face_f, turn_f, nbr_c, face_c, turn_c,
    w_time, w_vol, w_proj, w_rot, w_lift,
    state_f, state_c, stiff_v, vol_v, lift_v, project_v, rotate_v, lift_t,
    d_fine, t_fine, d_coarse, t_coarse, sems,
):
    moves = [
        (stiff, stiff_v), (fine_state, state_f), (fine_star, star_f), (coarse_state, state_c),
        (coarse_star, star_c), (send_fine, send_f), (send_coarse, send_c),
        (stiff_volume, vol_v), (lift, lift_v), (project, project_v), (rotate, rotate_v),
        (neighbors, nbr_f), (faces, face_f), (turns, turn_f),
        (c_neighbors, nbr_c), (c_faces, face_c), (c_turns, turn_c),
        (fine_flux, flux_f), (coarse_flux, flux_c),
    ]
    copies = [pltpu.make_async_copy(s, d, sems.at[i]) for i, (s, d) in enumerate(moves)]
    for copy in copies:
        copy.start()
    copies[0].wait()
    fill_weight(w_time, [stiff_v[d] for d in range(3)], BP, BP)
    w = weight(w_time, BP)

    def emit_coarse(tile, *terms):
        put(c_first, combine(FIRST_HALF, *terms), 2 * LANES, tile)
        put(c_second, combine(SECOND_HALF, *terms), 2 * LANES, tile)

    live = lax.broadcasted_iota(I32, (BP, LANES), 1) < count[0]

    def emit_fine(tile, *terms):
        values = combine(FIRST_HALF, *terms)
        put(i_fine, [jnp.where(live, v, 0.0) for v in values], LANES, tile)

    copies[1].wait()
    load_state(state_f, x_fine, LANES)
    t_fine[...] = mm(w, x_fine[...])
    copies[3].wait()
    load_state(state_c, x_coarse, 2 * LANES)
    t_coarse[...] = mm(w, x_coarse[...])
    copies[2].wait()
    first_term(x_fine, d_fine, t_fine, star_f, LANES)
    t_fine[...] = mm(w, d_fine[...])
    copies[4].wait()
    first_term(x_coarse, d_coarse, t_coarse, star_c, 2 * LANES)
    t_coarse[...] = mm(w, d_coarse[...])
    second_term(x_fine, d_fine, t_fine, star_f, LANES, emit_fine)
    second_term(x_coarse, d_coarse, t_coarse, star_c, 2 * LANES, emit_coarse)
    for copy in copies[5:11]:
        copy.wait()
    fill_weight(w_vol, [vol_v[d] for d in range(3)], BP, BP)
    fill_weight(w_proj, [project_v[:, f, :] for f in range(4)], FP, BP)
    w_rot[...] = jnp.zeros(w_rot.shape, F32)
    for h in range(3):
        w_rot[h * FP : h * FP + FNB, 0:FNB] = rotate_v[h]
    lift_t[...] = jnp.zeros(lift_t.shape, F32)
    for i in range(4):
        lift_t[i * FP : i * FP + FNB, 0:NB] = lift_v[:, i, :]
    hi, lo = halves(lift_t[...].T[0:BP, 0:32])
    w_lift[...] = jnp.zeros(w_lift.shape, F32)
    w_lift[:, 0:32] = hi
    w_lift[:, 32:64] = hi
    w_lift[:, 64:96] = lo
    pack(keep, swap, i_fine, c_first, send_f, send_c)
    for copy in copies[11:]:
        copy.wait()


def locate(n):
    me, chip, core = place()
    local = n < 384
    fine = n < 480
    g = jnp.where(fine, n - 384, n - 480)
    j = jnp.where(fine, g >> 3, g >> 2)
    s = jnp.where(fine, g & 7, g & 3)
    offset = j - REACH + jnp.where(j >= REACH, 1, 0)
    source = me - offset
    away = (source >> 1) - chip
    apart = jnp.abs(away)
    ahead = 1 - 2 * core
    direct = away * ahead < 0
    other = (source & 1) ^ core
    block = 2 * (apart - 1) + jnp.where(direct, other, 7 - other)
    block = jnp.where(away == 0, 12, block)
    lane = jnp.where(local, n & 127, block * 8 + s)
    tile = jnp.where(local, n >> 7, jnp.where(fine, 3, 4))
    return tile, lane


def spread(row_ref, i, tile):
    return jnp.broadcast_to(row_ref[i : i + 1, tile * LANES : (tile + 1) * LANES], (8, LANES))


def pick(options, bits):
    if len(options) == 1:
        return options[0]
    pairs = [options[i : i + 2] for i in range(0, len(options), 2)]
    merged = [jnp.where(bits[0], p[1], p[0]) if len(p) == 2 else p[0] for p in pairs]
    return pick(merged, bits[1:])


def bits_of(number, count):
    return [(number & (1 << k)) != 0 for k in range(count)]


def at_face(tables, firsts, q, at, numbers):
    found = []
    for (ref, width, tile), first in zip(tables, firsts):
        start = first(q) * width + tile * LANES
        found.append(pick([
            jnp.take_along_axis(ref[f * FP : (f + 1) * FP, start : start + LANES], at, axis=1)
            for f in range(4)
        ], numbers))
    return found


def near_part(
    state_ref, width, own_ref, tables, neighbors, faces, star_ref, flux_ref, t_ref,
    base_ref, side_ref, near_ref,
):
    for tile in range(width // LANES):
        lanes = slice(tile * LANES, (tile + 1) * LANES)
        for i in range(4):
            kind, lane = locate(spread(neighbors, i, tile))
            kinds = bits_of(kind, 2)
            numbers = bits_of(spread(faces, i, tile), 2)
            acc = [None] * NQ
            for q in range(NQ):
                start = q * width + tile * LANES
                found = at_face(tables, [lambda q: q] * 3, q, lane, numbers)
                near_ref[i, :, start : start + LANES] = pick(found, kinds)
                own = own_ref[i * FP : (i + 1) * FP, start : start + LANES]
                for p in range(NQ):
                    term = own * flux_ref[0, q, p, i : i + 1, lanes]
                    acc[p] = term if acc[p] is None else acc[p] + term
            for p in range(NQ):
                start = p * width + tile * LANES
                side_ref[i * FP : (i + 1) * FP, start : start + LANES] = acc[p]
        volume = star_sum(t_ref, star_ref, width, tile)
        state = get(state_ref, width, tile)
        put(base_ref, [s + v for s, v in zip(state, volume)], width, tile)


def far_part(
    width, ghosts, neighbors, faces, turns, flux_ref, w_rot, w_lift,
    base_ref, side_ref, near_ref, n_ref, l_ref, emit,
):
    turned = [
        [jnp.broadcast_to(w_rot[h * FP : (h + 1) * FP, b : b + 1], (FP, LANES)) for h in range(3)]
        for b in range(FNB)
    ]
    for tile in range(width // LANES):
        lanes = slice(tile * LANES, (tile + 1) * LANES)
        for i in range(4):
            kind, lane = locate(spread(neighbors, i, tile))
            later = jnp.where(kind == 4, lane + 4, lane)
            fine, local = kind == 3, kind < 3
            numbers = bits_of(spread(faces, i, tile), 2)
            for q in range(NQ):
                start = q * width + tile * LANES
                found = at_face(
                    ghosts, [lambda q: q, lambda q: q % 5], q, lane if q < 5 else later, numbers
                )
                ghost = jnp.where(fine, found[0], found[1])
                n_ref[i, :, q * LANES : (q + 1) * LANES] = jnp.where(
                    local, near_ref[i, :, start : start + LANES], ghost
                )
            ways = bits_of(spread(turns, i, tile), 2)
            turn_by = [pick(turned[b], ways) for b in range(FNB)]
            acc = []
            for p in range(NQ):
                start = p * width + tile * LANES
                acc.append(side_ref[i * FP : (i + 1) * FP, start : start + LANES])
            for q in range(NQ):
                at = slice(q * LANES, (q + 1) * LANES)
                other = turn_by[0] * n_ref[i, 0:1, at]
                for b in range(1, FNB):
                    other = other + turn_by[b] * n_ref[i, b : b + 1, at]
                for p in range(NQ):
                    acc[p] = acc[p] + other * flux_ref[1, q, p, i : i + 1, lanes]
            for p in range(NQ):
                l_ref[i * FP : (i + 1) * FP, p * LANES : (p + 1) * LANES] = acc[p]
        lifted = mm(w_lift, l_ref[...])
        base = get(base_ref, width, tile)
        emit(tile, [base[p] + lifted[:, p * LANES : (p + 1) * LANES] for p in range(NQ)])


def near_fine_kernel(
    sibling, x_fine, i_fine, c_first, star_f, flux_f, neighbors, faces, w_vol, w_proj,
    base, side, near, p_own, p_coarse, spare,
    t_ref,
):
    spare[...] = sibling[KEPT : KEPT + 8]
    w_v, w_p = weight(w_vol, BP), weight(w_proj, BP)
    t_ref[...] = mm(w_v, i_fine[...])
    p_own[...] = mm(w_p, i_fine[...])
    p_coarse[...] = mm(w_p, c_first[...])
    tables = [(p_own, LANES, 0), (p_coarse, 2 * LANES, 0), (p_coarse, 2 * LANES, 1)]
    near_part(
        x_fine, LANES, p_own, tables, neighbors, faces, star_f, flux_f, t_ref, base, side, near,
    )


def near_last_kernel(
    sibling, x_fine, i_fine, x_coarse, c_first, c_second, p_own, p_coarse,
    fine_star, fine_flux, coarse_star, coarse_flux, neighbors, faces, c_neighbors, c_faces,
    w_vol, w_proj,
    base_f, side_f, near_f, base_c, side_c, near_c, spare,
    q_own, q_coarse, t_ref, tc_ref,
):
    spare[...] = sibling[KEPT : KEPT + 8]
    w_v, w_p = weight(w_vol, BP), weight(w_proj, BP)
    t_ref[...] = mm(w_v, i_fine[...])
    q_own[...] = mm(w_p, i_fine[...])
    q_coarse[...] = mm(w_p, c_second[...])
    tc_ref[...] = mm(w_v, c_first[...] + c_second[...])
    tables = [(q_own, LANES, 0), (q_coarse, 2 * LANES, 0), (q_coarse, 2 * LANES, 1)]
    near_part(
        x_fine, LANES, q_own, tables, neighbors, faces, fine_star, fine_flux, t_ref,
        base_f, side_f, near_f,
    )
    q_own[...] = q_own[...] + p_own[...]
    q_coarse[...] = q_coarse[...] + p_coarse[...]
    near_part(
        x_coarse, 2 * LANES, q_coarse, tables, c_neighbors, c_faces, coarse_star, coarse_flux,
        tc_ref, base_c, side_c, near_c,
    )


def second_kernel(
    got_1, got_2, got_3, back, sibling, x_fine, base, side, near, c_second, star_f, flux_f,
    neighbors, faces, turns, send_fine, send_coarse, w_time, w_proj, w_rot, w_lift, count,
    keep, swap, x_next, i_next, p_gf, p_gc,
    ghost_f, ghost_c, t_ref, n_ref, l_ref, d_ref,
):
    w_p = weight(w_proj, BP)
    unpack((got_1, got_2, got_3, back, sibling), ghost_f, ghost_c)
    p_gf[...] = mm(w_p, ghost_f[...])
    p_gc[...] = mm(w_p, ghost_c[...])
    live = lax.broadcasted_iota(I32, (BP, LANES), 1) < count[0]

    def emit_state(tile, values):
        old = get(x_fine, LANES, 0)
        put(x_next, [jnp.where(live, v, o) for v, o in zip(values, old)], LANES, 0)

    far_part(
        LANES, [(p_gf, LANES, 0), (p_gc, LANES, 0)], neighbors, faces, turns, flux_f,
        w_rot, weight(w_lift, 32), base, side, near, n_ref, l_ref, emit_state,
    )

    def emit_fine(tile, *terms):
        values = combine(FIRST_HALF, *terms)
        put(i_next, [jnp.where(live, v, 0.0) for v in values], LANES, 0)

    w = weight(w_time, BP)
    t_ref[...] = mm(w, x_next[...])
    first_term(x_next, d_ref, t_ref, star_f, LANES)
    t_ref[...] = mm(w, d_ref[...])
    second_term(x_next, d_ref, t_ref, star_f, LANES, emit_fine)
    pack(keep, swap, i_next, c_second, send_fine, send_coarse)


def third_kernel(
    got_1, got_2, got_3, back, sibling, x_fine, base_f, side_f, near_f, base_c, side_c, near_c,
    p_gf, p_gc, fine_flux, coarse_flux, neighbors, faces, turns, c_neighbors, c_faces, c_turns,
    w_proj, w_rot, w_lift, count,
    fine_out, coarse_out,
    q_gf, q_gc, ghost_f, ghost_c, n_ref, l_ref, fine_v, coarse_v, sems,
):
    w_p, w_l = weight(w_proj, BP), weight(w_lift, 32)
    unpack((got_1, got_2, got_3, back, sibling), ghost_f, ghost_c)
    q_gf[...] = mm(w_p, ghost_f[...])
    q_gc[...] = mm(w_p, ghost_c[...])
    live = lax.broadcasted_iota(I32, (NB, LANES), 1) < count[0]
    ghosts = [(q_gf, LANES, 0), (q_gc, LANES, 0)]

    def emit_fine(tile, values):
        old = get(x_fine, LANES, 0)
        for p in range(NQ):
            fine_v[p] = jnp.where(live, values[p][:NB], old[p][:NB])

    far_part(
        LANES, ghosts, neighbors, faces, turns, fine_flux, w_rot, w_l,
        base_f, side_f, near_f, n_ref, l_ref, emit_fine,
    )
    fine_copy = pltpu.make_async_copy(fine_v, fine_out, sems.at[0])
    fine_copy.start()
    q_gf[...] = q_gf[...] + p_gf[...]
    q_gc[...] = q_gc[...] + p_gc[...]

    def emit_coarse(tile, values):
        for p in range(NQ):
            coarse_v[p, :, tile * LANES : (tile + 1) * LANES] = values[p][:NB]

    far_part(
        2 * LANES, ghosts, c_neighbors, c_faces, c_turns, coarse_flux, w_rot, w_l,
        base_c, side_c, near_c, n_ref, l_ref, emit_coarse,
    )
    coarse_copy = pltpu.make_async_copy(coarse_v, coarse_out, sems.at[1])
    coarse_copy.start()
    fine_copy.wait()
    coarse_copy.wait()


VM = pl.BlockSpec(memory_space=pltpu.VMEM)
SM = pl.BlockSpec(memory_space=pltpu.SMEM)
ANY = pl.BlockSpec(memory_space=pltpu.HBM)

FINE = (BP, NQ * LANES)
COARSE = (BP, 2 * NQ * LANES)
FACES_F = (4 * FP, NQ * LANES)
FACES_C = (4 * FP, 2 * NQ * LANES)
STIFF_F = (3 * BP, NQ * LANES)
STIFF_C = (3 * BP, 2 * NQ * LANES)
GHOST_C = (BP, 5 * LANES)
FACES_G = (4 * FP, 5 * LANES)
PICKED = (4, FP, NQ * LANES)
PICKED_C = (4, FP, 2 * NQ * LANES)
WEIGHTS = [(3 * BP, LANES), (4 * FP, LANES), (3 * FP, LANES), (BP, LANES)]
PARAMS = pltpu.CompilerParams(vmem_limit_bytes=24 * 1024 * 1024)


def call(kernel, name, outs, scratches, args, count, hbm_in=False, hbm_out=False, sems=0, us=2):
    if hbm_in:
        args = [pltpu.with_memory_space_constraint(a, pltpu.HBM) for a in args]
    kinds = [pltpu.VMEM(s, F32) if isinstance(s, tuple) else s for s in scratches]
    if sems:
        kinds.append(pltpu.SemaphoreType.DMA((sems,)))
    return pl.pallas_call(
        kernel,
        name=name,
        in_specs=[ANY if hbm_in else VM] * len(args) + [SM] * len(count),
        out_specs=[ANY if hbm_out else VM] * len(outs),
        out_shape=[jax.ShapeDtypeStruct(s, F32) if isinstance(s, tuple) else s for s in outs],
        scratch_shapes=kinds,
        compiler_params=PARAMS,
        cost_estimate=pl.CostEstimate(flops=us * 10**9, bytes_accessed=us * 10**6, transcendentals=0),
    )(*args, *count)


SIBLING = [(i, i ^ 1) for i in range(N_DEV)]


def ahead_by(distance):
    pairs = []
    for i in range(N_DEV):
        target = i + (2 * distance if i % 2 == 0 else -2 * distance)
        pairs.append((i, target if 0 <= target < N_DEV else i ^ 1))
    return pairs


def exchange(keep, sibling, spare):
    sent = [jnp.concatenate([keep[16 * d : 16 * d + 16], sibling[16 * d : 16 * d + 16]]) for d in range(3)]
    got = [None] * 3
    for d in (2, 1, 0):
        got[d] = lax.ppermute(sent[d], "dom", ahead_by(d + 1))
    rest = [g.reshape(2, 2, 8, ROW)[:, 1].reshape(16, ROW) for g in got]
    back = lax.ppermute(jnp.concatenate(rest + [spare]), "dom", SIBLING)
    return *got, back, sibling


def local(
    fine_state, coarse_state, fine_star, coarse_star, fine_flux, coarse_flux,
    fine_neighbors, fine_faces, fine_turns, coarse_neighbors, coarse_faces, coarse_turns,
    fine_count, send_fine, send_coarse,
    stiff_time, stiff_volume, face_lift, face_project, face_rotate,
):
    fine_state, coarse_state = [s.transpose(1, 0, 2) for s in (fine_state, coarse_state)]
    fine_star, coarse_star = [s.transpose(1, 2, 0, 3) for s in (fine_star, coarse_star)]
    fine_flux, coarse_flux = [s.transpose(0, 2, 3, 1, 4) for s in (fine_flux, coarse_flux)]
    send_fine, send_coarse = [s.transpose(0, 2, 1) for s in (send_fine, send_coarse)]
    face_lift = face_lift.transpose(2, 0, 1)
    face_project = face_project.transpose(1, 0, 2)
    count = (fine_count,)
    links = (fine_neighbors, fine_faces, fine_turns, coarse_neighbors, coarse_faces, coarse_turns)
    fixed = (stiff_volume, face_lift, face_project, face_rotate)
    (keep, swap, x_fine, i_first, x_coarse, c_first, c_second, fine_star, coarse_star,
     send_fine, send_coarse, fine_flux, coarse_flux, *rest) = call(
        first_kernel, "predict",
        [(KEPT, ROW), (KEPT + 8, ROW), FINE, FINE, COARSE, COARSE, COARSE, fine_star.shape, coarse_star.shape]
        + [jax.ShapeDtypeStruct(s.shape, I32) for s in (send_fine, send_coarse)]
        + [fine_flux.shape, coarse_flux.shape]
        + [jax.ShapeDtypeStruct(s.shape, I32) for s in links]
        + WEIGHTS[:1] + WEIGHTS,
        [fine_state.shape, coarse_state.shape, stiff_time.shape] + [f.shape for f in fixed]
        + [(LANES, LANES), FINE, STIFF_F, COARSE, STIFF_C],
        (fine_state, coarse_state, fine_star, coarse_star, send_fine, send_coarse, stiff_time,
         fine_flux, coarse_flux, *links, *fixed),
        count, hbm_in=True, sems=19,
    )
    links, (w_time, *weights) = rest[:6], rest[6:]
    w_vol, w_proj, w_rot, w_lift = weights
    sibling = lax.ppermute(swap, "dom", SIBLING)
    base, side, near, p_own, p_coarse, spare = call(
        near_fine_kernel, "near_fine", [FINE, FACES_F, PICKED, FACES_F, FACES_C, (8, ROW)], [STIFF_F],
        (sibling, x_fine, i_first, c_first, fine_star, fine_flux, *links[:2], w_vol, w_proj), (), us=1,
    )
    arrived = exchange(keep, sibling, spare)
    keep, swap, x_next, i_second, p_gf, p_gc = call(
        second_kernel, "substep",
        [(KEPT, ROW), (KEPT + 8, ROW), FINE, FINE, FACES_F, FACES_G],
        [FINE, GHOST_C, STIFF_F, PICKED, FACES_F, FINE],
        (*arrived, x_fine, base, side, near, c_second, fine_star, fine_flux, *links[:3],
         send_fine, send_coarse, w_time, w_proj, w_rot, w_lift), count,
    )
    sibling = lax.ppermute(swap, "dom", SIBLING)
    *near_parts, spare = call(
        near_last_kernel, "near_last",
        [FINE, FACES_F, PICKED, COARSE, FACES_C, PICKED_C, (8, ROW)],
        [FACES_F, FACES_C, STIFF_F, STIFF_C],
        (sibling, x_next, i_second, x_coarse, c_first, c_second, p_own, p_coarse,
         fine_star, fine_flux, coarse_star, coarse_flux, *links[:2], *links[3:5], w_vol, w_proj),
        (), us=2,
    )
    arrived = exchange(keep, sibling, spare)
    results = call(
        third_kernel, "finish",
        [(NQ, NB, LANES), (NQ, NB, 2 * LANES)],
        [FACES_F, FACES_G, FINE, GHOST_C, PICKED, FACES_F, (NQ, NB, LANES), (NQ, NB, 2 * LANES)],
        (*arrived, x_next, *near_parts, p_gf, p_gc, fine_flux, coarse_flux, *links,
         w_proj, w_rot, w_lift), count,
        hbm_out=True, sems=2,
    )
    return tuple(r.transpose(1, 0, 2) for r in results)


def solution(mesh):
    placed = (
        P(None, None, "dom"),
        P(None, None, "dom"),
        P(None, None, None, "dom"),
        P(None, None, None, "dom"),
        P(None, None, None, None, "dom"),
        P(None, None, None, None, "dom"),
        P(None, "dom"),
        P(None, "dom"),
        P(None, "dom"),
        P(None, "dom"),
        P(None, "dom"),
        P(None, "dom"),
        P("dom"),
        P("dom", None, None),
        P("dom", None, None),
        P(),
        P(),
        P(),
        P(),
        P(),
    )
    return jax.shard_map(
        local,
        mesh=mesh,
        in_specs=placed,
        out_specs=(P(None, None, "dom"), P(None, None, "dom")),
        check_vma=False,
    )
```

```python
from functools import partial

import jax
import jax.numpy as jnp
from jax import lax
from jax.experimental import pallas as pl
from jax.experimental.pallas import tpu as pltpu
from jax.sharding import PartitionSpec as P

NB = 20
NQ = 9
FNB = 6
REACH = 6
BP = 24
FP = 8
LANES = 128
ROW = 384
FIRST_HALF = (0.5, 0.125, 1.0 / 48.0)
SECOND_HALF = (0.5, 0.375, 7.0 / 48.0)
F32 = jnp.float32
BF16 = jnp.bfloat16
I32 = jnp.int32
N_DEV = 128
BLOCKS = 13
KEPT = 48


def halves(x):
    hi = x.astype(BF16).astype(F32)
    return hi, x - hi


def stacked(x):
    hi, lo = halves(x)
    return jnp.concatenate([hi, lo, hi], axis=0).astype(BF16)


def fill_weight(ref, blocks, row_step, col_step):
    ref[...] = jnp.zeros(ref.shape, F32)
    for i, block in enumerate(blocks):
        rows, cols = block.shape
        hi, lo = halves(block)
        span = slice(i * row_step, i * row_step + rows)
        ref[span, 0:cols] = hi
        ref[span, col_step : col_step + cols] = hi
        ref[span, 2 * col_step : 2 * col_step + cols] = lo


def weight(ref, depth):
    return ref[:, 0 : 3 * depth].astype(BF16)


def mm(w, x):
    return jnp.dot(w, stacked(x), preferred_element_type=F32)


def load_state(state_ref, x_ref, width):
    for q in range(NQ):
        x_ref[NB:BP, q * width : (q + 1) * width] = jnp.zeros((BP - NB, width), F32)
        x_ref[0:NB, q * width : (q + 1) * width] = state_ref[q]


def star_sum(t_ref, star_ref, width, tile):
    lanes = slice(tile * LANES, (tile + 1) * LANES)
    acc = [None] * NQ
    for q in range(NQ):
        for d in range(3):
            t = t_ref[d * BP : (d + 1) * BP, q * width + tile * LANES : q * width + (tile + 1) * LANES]
            for p in range(NQ):
                term = t * star_ref[q, p, d : d + 1, lanes]
                acc[p] = term if acc[p] is None else acc[p] + term
    return acc


def put(ref, values, width, tile):
    for p in range(NQ):
        ref[:, p * width + tile * LANES : p * width + (tile + 1) * LANES] = values[p]


def get(ref, width, tile):
    return [
        ref[:, p * width + tile * LANES : p * width + (tile + 1) * LANES] for p in range(NQ)
    ]


def first_term(x_ref, d_ref, t_ref, star_ref, width):
    for tile in range(width // LANES):
        put(d_ref, star_sum(t_ref, star_ref, width, tile), width, tile)


def second_term(x_ref, d_ref, t_ref, star_ref, width, emit):
    for tile in range(width // LANES):
        second = star_sum(t_ref, star_ref, width, tile)
        emit(tile, get(x_ref, width, tile), get(d_ref, width, tile), second)


def combine(weights, state, neg_first, second):
    return [
        weights[0] * s - weights[1] * f + weights[2] * g
        for s, f, g in zip(state, neg_first, second)
    ]


def place():
    me = lax.axis_index("dom").astype(I32)
    return me, me >> 1, me & 1


def route(block):
    me, chip, core = place()
    if block == 12:
        offset = 1 - 2 * core
    else:
        sender = core if block < 6 else 1 - core
        ahead = 1 - 2 * sender
        distance = (block % 6) // 2 + 1
        offset = 2 * ahead * distance + (sender ^ (block % 2)) - core
    target = me + offset
    valid = (target >= 0) & (target < N_DEV) & (offset >= -REACH) & (offset <= REACH)
    peer = jnp.where(offset < 0, offset + REACH, offset + REACH - 1)
    return jnp.where(valid, peer, -1)


def picker(send_ref, slots):
    table = send_ref[0].astype(F32) + 1.0
    if table.shape[0] < 8:
        table = jnp.concatenate([table, table], axis=0)
    lane = lax.broadcasted_iota(I32, table.shape, 1)
    rows = []
    for block in range(BLOCKS):
        rows.append(jnp.where(lane == route(block), table, 0.0))
    index = jnp.sum(jnp.concatenate(rows, axis=0), axis=1, keepdims=True)
    slot = lax.broadcasted_iota(I32, (BLOCKS * 8, slots), 1).astype(F32)
    return jnp.where(slot + 1.0 == index, 1.0, 0.0).astype(BF16)


def rows_of(ref, width, first, last):
    return jnp.concatenate([ref[:, q * width : (q + 1) * width] for q in range(first, last)], axis=0)


def picked(hot, field):
    hi, lo = halves(field)
    both = jnp.concatenate([hi, lo], axis=1).astype(BF16)
    hots = jnp.concatenate([hot, hot], axis=1)
    return lax.dot_general(hots, both, (((1,), (1,)), ((), ())), preferred_element_type=F32)


def pack(keep_ref, swap_ref, fine_ref, coarse_ref, send_fine_ref, send_coarse_ref):
    fine = picked(picker(send_fine_ref, LANES), rows_of(fine_ref, LANES, 0, NQ))
    hot = picker(send_coarse_ref, 2 * LANES)
    low = picked(hot, rows_of(coarse_ref, 2 * LANES, 0, 5))
    high = picked(hot, rows_of(coarse_ref, 2 * LANES, 5, NQ))
    high = jnp.concatenate([high, jnp.zeros((BLOCKS * 8, BP), F32)], axis=1)
    s = lax.broadcasted_iota(I32, (BLOCKS * 8, 5 * BP), 0) & 7
    coarse = jnp.where(s < 4, low, high)
    for ref, rows in ((keep_ref, slice(0, KEPT)), (swap_ref, slice(KEPT, BLOCKS * 8))):
        ref[:, 128:ROW] = jnp.zeros((ref.shape[0], ROW - LANES), F32)
        ref[:, 0 : NQ * BP] = fine[rows]
        ref[:, 256 : 256 + 5 * BP] = coarse[rows]


def unpack(arrived, fine_ref, coarse_ref):
    *direct, back, sibling = arrived
    parts = []
    for ref in direct:
        parts += [ref[0:8], ref[16:24]]
    parts += [back[0:KEPT], sibling[KEPT : KEPT + 8], jnp.zeros((LANES - BLOCKS * 8, ROW), F32)]
    rows = jnp.concatenate(parts, axis=0)
    turned = [rows[:, t * LANES : (t + 1) * LANES].T for t in range(3)]
    fine = jnp.concatenate(turned[:2], axis=0)
    for q in range(NQ):
        fine_ref[:, q * LANES : (q + 1) * LANES] = fine[q * BP : (q + 1) * BP]
    for q in range(5):
        coarse_ref[:, q * LANES : (q + 1) * LANES] = turned[2][q * BP : (q + 1) * BP]


def first_kernel(
    fine_state, coarse_state, fine_star, coarse_star, send_fine, send_coarse, stiff,
    fine_flux, coarse_flux, neighbors, faces, turns, c_neighbors, c_faces, c_turns,
    stiff_volume, lift, project, rotate, count,
    keep, swap, x_fine, i_fine, x_coarse, c_first, c_second, star_f, star_c, send_f, send_c,
    flux_f, flux_c, nbr_f, face_f, turn_f, nbr_c, face_c, turn_c,
    w_time, w_vol, w_proj, w_rot, w_lift,
    state_f, state_c, stiff_v, vol_v, lift_v, project_v, rotate_v, lift_t,
    d_fine, t_fine, d_coarse, t_coarse, sems,
):
    moves = [
        (stiff, stiff_v), (fine_state, state_f), (fine_star, star_f), (coarse_state, state_c),
        (coarse_star, star_c), (send_fine, send_f), (send_coarse, send_c),
        (stiff_volume, vol_v), (lift, lift_v), (project, project_v), (rotate, rotate_v),
        (neighbors, nbr_f), (faces, face_f), (turns, turn_f),
        (c_neighbors, nbr_c), (c_faces, face_c), (c_turns, turn_c),
        (fine_flux, flux_f), (coarse_flux, flux_c),
    ]
    copies = [pltpu.make_async_copy(s, d, sems.at[i]) for i, (s, d) in enumerate(moves)]
    for copy in copies:
        copy.start()
    copies[0].wait()
    fill_weight(w_time, [stiff_v[d] for d in range(3)], BP, BP)
    w = weight(w_time, BP)

    def emit_coarse(tile, *terms):
        put(c_first, combine(FIRST_HALF, *terms), 2 * LANES, tile)
        put(c_second, combine(SECOND_HALF, *terms), 2 * LANES, tile)

    live = lax.broadcasted_iota(I32, (BP, LANES), 1) < count[0]

    def emit_fine(tile, *terms):
        values = combine(FIRST_HALF, *terms)
        put(i_fine, [jnp.where(live, v, 0.0) for v in values], LANES, tile)

    copies[1].wait()
    load_state(state_f, x_fine, LANES)
    t_fine[...] = mm(w, x_fine[...])
    copies[3].wait()
    load_state(state_c, x_coarse, 2 * LANES)
    t_coarse[...] = mm(w, x_coarse[...])
    copies[2].wait()
    first_term(x_fine, d_fine, t_fine, star_f, LANES)
    t_fine[...] = mm(w, d_fine[...])
    copies[4].wait()
    first_term(x_coarse, d_coarse, t_coarse, star_c, 2 * LANES)
    t_coarse[...] = mm(w, d_coarse[...])
    second_term(x_fine, d_fine, t_fine, star_f, LANES, emit_fine)
    second_term(x_coarse, d_coarse, t_coarse, star_c, 2 * LANES, emit_coarse)
    for copy in copies[5:11]:
        copy.wait()
    fill_weight(w_vol, [vol_v[d] for d in range(3)], BP, BP)
    fill_weight(w_proj, [project_v[:, f, :] for f in range(4)], FP, BP)
    w_rot[...] = jnp.zeros(w_rot.shape, F32)
    for h in range(3):
        w_rot[h * FP : h * FP + FNB, 0:FNB] = rotate_v[h]
    lift_t[...] = jnp.zeros(lift_t.shape, F32)
    for i in range(4):
        lift_t[i * FP : i * FP + FNB, 0:NB] = lift_v[:, i, :]
    hi, lo = halves(lift_t[...].T[0:BP, 0:32])
    w_lift[...] = jnp.zeros(w_lift.shape, F32)
    w_lift[:, 0:32] = hi
    w_lift[:, 32:64] = hi
    w_lift[:, 64:96] = lo
    pack(keep, swap, i_fine, c_first, send_f, send_c)
    for copy in copies[11:]:
        copy.wait()


def locate(n):
    me, chip, core = place()
    local = n < 384
    fine = n < 480
    g = jnp.where(fine, n - 384, n - 480)
    j = jnp.where(fine, g >> 3, g >> 2)
    s = jnp.where(fine, g & 7, g & 3)
    offset = j - REACH + jnp.where(j >= REACH, 1, 0)
    source = me - offset
    away = (source >> 1) - chip
    apart = jnp.abs(away)
    ahead = 1 - 2 * core
    direct = away * ahead < 0
    other = (source & 1) ^ core
    block = 2 * (apart - 1) + jnp.where(direct, other, 7 - other)
    block = jnp.where(away == 0, 12, block)
    lane = jnp.where(local, n & 127, block * 8 + s)
    tile = jnp.where(local, n >> 7, jnp.where(fine, 3, 4))
    return tile, lane


def spread(row_ref, i, tile):
    return jnp.broadcast_to(row_ref[i : i + 1, tile * LANES : (tile + 1) * LANES], (8, LANES))


def pick(options, bits):
    if len(options) == 1:
        return options[0]
    pairs = [options[i : i + 2] for i in range(0, len(options), 2)]
    merged = [jnp.where(bits[0], p[1], p[0]) if len(p) == 2 else p[0] for p in pairs]
    return pick(merged, bits[1:])


def bits_of(number, count):
    return [(number & (1 << k)) != 0 for k in range(count)]


def at_face(tables, firsts, q, at, numbers):
    found = []
    for (ref, width, tile), first in zip(tables, firsts):
        start = first(q) * width + tile * LANES
        found.append(pick([
            jnp.take_along_axis(ref[f * FP : (f + 1) * FP, start : start + LANES], at, axis=1)
            for f in range(4)
        ], numbers))
    return found


def near_part(
    state_ref, width, own_ref, tables, neighbors, faces, star_ref, flux_ref, t_ref,
    base_ref, side_ref, near_ref,
):
    for tile in range(width // LANES):
        lanes = slice(tile * LANES, (tile + 1) * LANES)
        for i in range(4):
            kind, lane = locate(spread(neighbors, i, tile))
            kinds = bits_of(kind, 2)
            numbers = bits_of(spread(faces, i, tile), 2)
            acc = [None] * NQ
            for q in range(NQ):
                start = q * width + tile * LANES
                found = at_face(tables, [lambda q: q] * 3, q, lane, numbers)
                near_ref[i, :, start : start + LANES] = pick(found, kinds)
                own = own_ref[i * FP : (i + 1) * FP, start : start + LANES]
                for p in range(NQ):
                    term = own * flux_ref[0, q, p, i : i + 1, lanes]
                    acc[p] = term if acc[p] is None else acc[p] + term
            for p in range(NQ):
                start = p * width + tile * LANES
                side_ref[i * FP : (i + 1) * FP, start : start + LANES] = acc[p]
        volume = star_sum(t_ref, star_ref, width, tile)
        state = get(state_ref, width, tile)
        put(base_ref, [s + v for s, v in zip(state, volume)], width, tile)


def far_part(
    width, ghosts, neighbors, faces, turns, flux_ref, w_rot, w_lift,
    base_ref, side_ref, near_ref, n_ref, l_ref, emit,
):
    turned = [
        [jnp.broadcast_to(w_rot[h * FP : (h + 1) * FP, b : b + 1], (FP, LANES)) for h in range(3)]
        for b in range(FNB)
    ]
    for tile in range(width // LANES):
        lanes = slice(tile * LANES, (tile + 1) * LANES)
        for i in range(4):
            kind, lane = locate(spread(neighbors, i, tile))
            later = jnp.where(kind == 4, lane + 4, lane)
            fine, local = kind == 3, kind < 3
            numbers = bits_of(spread(faces, i, tile), 2)
            for q in range(NQ):
                start = q * width + tile * LANES
                found = at_face(
                    ghosts, [lambda q: q, lambda q: q % 5], q, lane if q < 5 else later, numbers
                )
                ghost = jnp.where(fine, found[0], found[1])
                n_ref[i, :, q * LANES : (q + 1) * LANES] = jnp.where(
                    local, near_ref[i, :, start : start + LANES], ghost
                )
            ways = bits_of(spread(turns, i, tile), 2)
            turn_by = [pick(turned[b], ways) for b in range(FNB)]
            acc = []
            for p in range(NQ):
                start = p * width + tile * LANES
                acc.append(side_ref[i * FP : (i + 1) * FP, start : start + LANES])
            for q in range(NQ):
                at = slice(q * LANES, (q + 1) * LANES)
                other = turn_by[0] * n_ref[i, 0:1, at]
                for b in range(1, FNB):
                    other = other + turn_by[b] * n_ref[i, b : b + 1, at]
                for p in range(NQ):
                    acc[p] = acc[p] + other * flux_ref[1, q, p, i : i + 1, lanes]
            for p in range(NQ):
                l_ref[i * FP : (i + 1) * FP, p * LANES : (p + 1) * LANES] = acc[p]
        lifted = mm(w_lift, l_ref[...])
        base = get(base_ref, width, tile)
        emit(tile, [base[p] + lifted[0:BP, p * LANES : (p + 1) * LANES] for p in range(NQ)], lifted)


def near_fine_kernel(
    sibling, x_fine, i_fine, c_first, star_f, flux_f, neighbors, faces, w_vol, w_proj, w_time, w_lift,
    base, side, near, p_own, p_coarse, t_base, w_both, spare,
    t_ref,
):
    spare[...] = sibling[KEPT : KEPT + 8]
    w_v, w_p = weight(w_vol, BP), weight(w_proj, BP)
    t_ref[...] = mm(w_v, i_fine[...])
    p_own[...] = mm(w_p, i_fine[...])
    p_coarse[...] = mm(w_p, c_first[...])
    tables = [(p_own, LANES, 0), (p_coarse, 2 * LANES, 0), (p_coarse, 2 * LANES, 1)]
    near_part(
        x_fine, LANES, p_own, tables, neighbors, faces, star_f, flux_f, t_ref, base, side, near,
    )
    w = weight(w_time, BP)
    t_base[...] = mm(w, base[...])
    hi, lo = halves(mm(w, w_lift[:, 0:32] + w_lift[:, 64:96]))
    w_both[...] = jnp.zeros(w_both.shape, F32)
    w_both[0:BP, :] = w_lift[...]
    w_both[BP:, 0:32] = hi
    w_both[BP:, 32:64] = hi
    w_both[BP:, 64:96] = lo


def near_last_kernel(
    sibling, x_fine, i_fine, x_coarse, c_first, c_second, p_own, p_coarse,
    fine_star, fine_flux, coarse_star, coarse_flux, neighbors, faces, c_neighbors, c_faces,
    w_vol, w_proj,
    base_f, side_f, near_f, base_c, side_c, near_c, spare,
    q_own, q_coarse, t_ref, tc_ref,
):
    spare[...] = sibling[KEPT : KEPT + 8]
    w_v, w_p = weight(w_vol, BP), weight(w_proj, BP)
    t_ref[...] = mm(w_v, i_fine[...])
    q_own[...] = mm(w_p, i_fine[...])
    q_coarse[...] = mm(w_p, c_second[...])
    tc_ref[...] = mm(w_v, c_first[...] + c_second[...])
    tables = [(q_own, LANES, 0), (q_coarse, 2 * LANES, 0), (q_coarse, 2 * LANES, 1)]
    near_part(
        x_fine, LANES, q_own, tables, neighbors, faces, fine_star, fine_flux, t_ref,
        base_f, side_f, near_f,
    )
    q_own[...] = q_own[...] + p_own[...]
    q_coarse[...] = q_coarse[...] + p_coarse[...]
    near_part(
        x_coarse, 2 * LANES, q_coarse, tables, c_neighbors, c_faces, coarse_star, coarse_flux,
        tc_ref, base_c, side_c, near_c,
    )


def second_kernel(
    got_1, got_2, got_3, back, sibling, x_fine, base, side, near, t_base, c_second, star_f, flux_f,
    neighbors, faces, turns, send_fine, send_coarse, w_time, w_proj, w_rot, w_both, count,
    keep, swap, x_next, i_next, p_gf, p_gc,
    ghost_f, ghost_c, t_ref, n_ref, l_ref, d_ref,
):
    w_p = weight(w_proj, BP)
    unpack((got_1, got_2, got_3, back, sibling), ghost_f, ghost_c)
    p_gf[...] = mm(w_p, ghost_f[...])
    p_gc[...] = mm(w_p, ghost_c[...])
    live = lax.broadcasted_iota(I32, (BP, LANES), 1) < count[0]

    def emit_state(tile, values, lifted):
        t_ref[...] = t_base[...] + lifted[BP:]
        old = get(x_fine, LANES, 0)
        put(x_next, [jnp.where(live, v, o) for v, o in zip(values, old)], LANES, 0)

    far_part(
        LANES, [(p_gf, LANES, 0), (p_gc, LANES, 0)], neighbors, faces, turns, flux_f,
        w_rot, weight(w_both, 32), base, side, near, n_ref, l_ref, emit_state,
    )

    def emit_fine(tile, *terms):
        values = combine(FIRST_HALF, *terms)
        put(i_next, [jnp.where(live, v, 0.0) for v in values], LANES, 0)

    w = weight(w_time, BP)
    first_term(x_next, d_ref, t_ref, star_f, LANES)
    t_ref[...] = mm(w, d_ref[...])
    second_term(x_next, d_ref, t_ref, star_f, LANES, emit_fine)
    pack(keep, swap, i_next, c_second, send_fine, send_coarse)


def third_kernel(
    got_1, got_2, got_3, back, sibling, x_fine, base_f, side_f, near_f, base_c, side_c, near_c,
    p_gf, p_gc, fine_flux, coarse_flux, neighbors, faces, turns, c_neighbors, c_faces, c_turns,
    w_proj, w_rot, w_lift, count,
    fine_out, coarse_out,
    q_gf, q_gc, ghost_f, ghost_c, n_ref, l_ref, fine_v, coarse_v, sems,
):
    w_p, w_l = weight(w_proj, BP), weight(w_lift, 32)
    unpack((got_1, got_2, got_3, back, sibling), ghost_f, ghost_c)
    q_gf[...] = mm(w_p, ghost_f[...])
    q_gc[...] = mm(w_p, ghost_c[...])
    live = lax.broadcasted_iota(I32, (NB, LANES), 1) < count[0]
    ghosts = [(q_gf, LANES, 0), (q_gc, LANES, 0)]

    def emit_fine(tile, values, lifted):
        old = get(x_fine, LANES, 0)
        for p in range(NQ):
            fine_v[p] = jnp.where(live, values[p][:NB], old[p][:NB])

    far_part(
        LANES, ghosts, neighbors, faces, turns, fine_flux, w_rot, w_l,
        base_f, side_f, near_f, n_ref, l_ref, emit_fine,
    )
    fine_copy = pltpu.make_async_copy(fine_v, fine_out, sems.at[0])
    fine_copy.start()
    q_gf[...] = q_gf[...] + p_gf[...]
    q_gc[...] = q_gc[...] + p_gc[...]

    def emit_coarse(tile, values, lifted):
        for p in range(NQ):
            coarse_v[p, :, tile * LANES : (tile + 1) * LANES] = values[p][:NB]

    far_part(
        2 * LANES, ghosts, c_neighbors, c_faces, c_turns, coarse_flux, w_rot, w_l,
        base_c, side_c, near_c, n_ref, l_ref, emit_coarse,
    )
    coarse_copy = pltpu.make_async_copy(coarse_v, coarse_out, sems.at[1])
    coarse_copy.start()
    fine_copy.wait()
    coarse_copy.wait()


VM = pl.BlockSpec(memory_space=pltpu.VMEM)
SM = pl.BlockSpec(memory_space=pltpu.SMEM)
ANY = pl.BlockSpec(memory_space=pltpu.HBM)

FINE = (BP, NQ * LANES)
COARSE = (BP, 2 * NQ * LANES)
FACES_F = (4 * FP, NQ * LANES)
FACES_C = (4 * FP, 2 * NQ * LANES)
STIFF_F = (3 * BP, NQ * LANES)
STIFF_C = (3 * BP, 2 * NQ * LANES)
GHOST_C = (BP, 5 * LANES)
FACES_G = (4 * FP, 5 * LANES)
PICKED = (4, FP, NQ * LANES)
PICKED_C = (4, FP, 2 * NQ * LANES)
WEIGHTS = [(3 * BP, LANES), (4 * FP, LANES), (3 * FP, LANES), (BP, LANES)]
PARAMS = pltpu.CompilerParams(vmem_limit_bytes=24 * 1024 * 1024)


def call(kernel, name, outs, scratches, args, count, hbm_in=False, hbm_out=False, sems=0, us=2):
    if hbm_in:
        args = [pltpu.with_memory_space_constraint(a, pltpu.HBM) for a in args]
    kinds = [pltpu.VMEM(s, F32) if isinstance(s, tuple) else s for s in scratches]
    if sems:
        kinds.append(pltpu.SemaphoreType.DMA((sems,)))
    return pl.pallas_call(
        kernel,
        name=name,
        in_specs=[ANY if hbm_in else VM] * len(args) + [SM] * len(count),
        out_specs=[ANY if hbm_out else VM] * len(outs),
        out_shape=[jax.ShapeDtypeStruct(s, F32) if isinstance(s, tuple) else s for s in outs],
        scratch_shapes=kinds,
        compiler_params=PARAMS,
        cost_estimate=pl.CostEstimate(flops=us * 10**9, bytes_accessed=us * 10**6, transcendentals=0),
    )(*args, *count)


SIBLING = [(i, i ^ 1) for i in range(N_DEV)]


def ahead_by(distance):
    pairs = []
    for i in range(N_DEV):
        target = i + (2 * distance if i % 2 == 0 else -2 * distance)
        pairs.append((i, target if 0 <= target < N_DEV else i ^ 1))
    return pairs


def exchange(keep, sibling, spare):
    sent = [jnp.concatenate([keep[16 * d : 16 * d + 16], sibling[16 * d : 16 * d + 16]]) for d in range(3)]
    got = [None] * 3
    for d in (2, 1, 0):
        got[d] = lax.ppermute(sent[d], "dom", ahead_by(d + 1))
    rest = [g.reshape(2, 2, 8, ROW)[:, 1].reshape(16, ROW) for g in got]
    back = lax.ppermute(jnp.concatenate(rest + [spare]), "dom", SIBLING)
    return *got, back, sibling


def local(
    fine_state, coarse_state, fine_star, coarse_star, fine_flux, coarse_flux,
    fine_neighbors, fine_faces, fine_turns, coarse_neighbors, coarse_faces, coarse_turns,
    fine_count, send_fine, send_coarse,
    stiff_time, stiff_volume, face_lift, face_project, face_rotate,
):
    fine_state, coarse_state = [s.transpose(1, 0, 2) for s in (fine_state, coarse_state)]
    fine_star, coarse_star = [s.transpose(1, 2, 0, 3) for s in (fine_star, coarse_star)]
    fine_flux, coarse_flux = [s.transpose(0, 2, 3, 1, 4) for s in (fine_flux, coarse_flux)]
    send_fine, send_coarse = [s.transpose(0, 2, 1) for s in (send_fine, send_coarse)]
    face_lift = face_lift.transpose(2, 0, 1)
    face_project = face_project.transpose(1, 0, 2)
    count = (fine_count,)
    links = (fine_neighbors, fine_faces, fine_turns, coarse_neighbors, coarse_faces, coarse_turns)
    fixed = (stiff_volume, face_lift, face_project, face_rotate)
    (keep, swap, x_fine, i_first, x_coarse, c_first, c_second, fine_star, coarse_star,
     send_fine, send_coarse, fine_flux, coarse_flux, *rest) = call(
        first_kernel, "predict",
        [(KEPT, ROW), (KEPT + 8, ROW), FINE, FINE, COARSE, COARSE, COARSE, fine_star.shape, coarse_star.shape]
        + [jax.ShapeDtypeStruct(s.shape, I32) for s in (send_fine, send_coarse)]
        + [fine_flux.shape, coarse_flux.shape]
        + [jax.ShapeDtypeStruct(s.shape, I32) for s in links]
        + WEIGHTS[:1] + WEIGHTS,
        [fine_state.shape, coarse_state.shape, stiff_time.shape] + [f.shape for f in fixed]
        + [(LANES, LANES), FINE, STIFF_F, COARSE, STIFF_C],
        (fine_state, coarse_state, fine_star, coarse_star, send_fine, send_coarse, stiff_time,
         fine_flux, coarse_flux, *links, *fixed),
        count, hbm_in=True, sems=19,
    )
    links, (w_time, *weights) = rest[:6], rest[6:]
    w_vol, w_proj, w_rot, w_lift = weights
    sibling = lax.ppermute(swap, "dom", SIBLING)
    base, side, near, p_own, p_coarse, t_base, w_both, spare = call(
        near_fine_kernel, "near_fine",
        [FINE, FACES_F, PICKED, FACES_F, FACES_C, STIFF_F, (4 * BP, LANES), (8, ROW)], [STIFF_F],
        (sibling, x_fine, i_first, c_first, fine_star, fine_flux, *links[:2], w_vol, w_proj,
         w_time, w_lift), (), us=1,
    )
    arrived = exchange(keep, sibling, spare)
    keep, swap, x_next, i_second, p_gf, p_gc = call(
        second_kernel, "substep",
        [(KEPT, ROW), (KEPT + 8, ROW), FINE, FINE, FACES_F, FACES_G],
        [FINE, GHOST_C, STIFF_F, PICKED, FACES_F, FINE],
        (*arrived, x_fine, base, side, near, t_base, c_second, fine_star, fine_flux, *links[:3],
         send_fine, send_coarse, w_time, w_proj, w_rot, w_both), count,
    )
    sibling = lax.ppermute(swap, "dom", SIBLING)
    *near_parts, spare = call(
        near_last_kernel, "near_last",
        [FINE, FACES_F, PICKED, COARSE, FACES_C, PICKED_C, (8, ROW)],
        [FACES_F, FACES_C, STIFF_F, STIFF_C],
        (sibling, x_next, i_second, x_coarse, c_first, c_second, p_own, p_coarse,
         fine_star, fine_flux, coarse_star, coarse_flux, *links[:2], *links[3:5], w_vol, w_proj),
        (), us=2,
    )
    arrived = exchange(keep, sibling, spare)
    results = call(
        third_kernel, "finish",
        [(NQ, NB, LANES), (NQ, NB, 2 * LANES)],
        [FACES_F, FACES_G, FINE, GHOST_C, PICKED, FACES_F, (NQ, NB, LANES), (NQ, NB, 2 * LANES)],
        (*arrived, x_next, *near_parts, p_gf, p_gc, fine_flux, coarse_flux, *links,
         w_proj, w_rot, w_lift), count,
        hbm_out=True, sems=2,
    )
    return tuple(r.transpose(1, 0, 2) for r in results)


def solution(mesh):
    placed = (
        P(None, None, "dom"),
        P(None, None, "dom"),
        P(None, None, None, "dom"),
        P(None, None, None, "dom"),
        P(None, None, None, None, "dom"),
        P(None, None, None, None, "dom"),
        P(None, "dom"),
        P(None, "dom"),
        P(None, "dom"),
        P(None, "dom"),
        P(None, "dom"),
        P(None, "dom"),
        P("dom"),
        P("dom", None, None),
        P("dom", None, None),
        P(),
        P(),
        P(),
        P(),
        P(),
    )
    return jax.shard_map(
        local,
        mesh=mesh,
        in_specs=placed,
        out_specs=(P(None, None, "dom"), P(None, None, "dom")),
        check_vma=False,
    )
```
